512 devices in a mesh: seq: 128 (over x_hi, z, y), dp: 4 (over x_lo, core).
Axes of the slice: x: 4 (x_hi: 2, x_lo: 2; x = x_hi * 2 + x_lo), y: 8, z: 8, core: 2. Of those that a mesh axis runs over, the one named last changes fastest.
Arguments:
- teacher_query: bfloat16 [4, 32768, 512], P('dp', 'seq'), may hold values from -24 to 24
- teacher_key: bfloat16 [4, 32768, 512], P('dp', 'seq'), may hold values from -24 to 24
- student_query: bfloat16 [4, 32768, 512], P('dp', 'seq'), may hold values from -24 to 24
- student_key: bfloat16 [4, 32768, 512], P('dp', 'seq'), may hold values from -24 to 24
- segment_ids: int32 [4, 32768], P('dp'), may hold values from 0 to 36, never falling along the last dimension, each value on 1 to 1792 neighbouring positions
- head_weight: float32 [4], replicated, may hold values from 100 to 400
Outputs:
- query_grad: float32 [4, 32768, 512], P('dp', 'seq')
- key_grad: float32 [4, 32768, 512], P('dp', 'seq')
The draws below stay inside these ranges and needn't reach their ends.
Inputs may be any that keep to these rules, and one draw needn't show every extreme that they name: `segment_ids`: every document of a window spans at most 1792 positions, and one spans exactly 1792.
All inputs are finite; a program needn't handle non-finite values.
Results may differ from the reference program's by a relative error of at most 0.0025.
Values may be sent and summed in bfloat16 or wider, within the bound.
No kernel may reach another device: no remote copies, remote signals or barrier semaphores. Data moves between devices by JAX's collectives and lax.ppermute only.
A program may use at most 64 MiB of HBM per device.

```python
import math
import jax
import jax.numpy as jnp
import numpy as np
from jax import lax

HEADS = 4
HEAD_DIM = 128
TOK_DEV = 256
BAND = 8
WINDOW = 32768
MOST = 1792
DOCS = 4
RELW = 512


def drawn_field(key):
    return 1.2 * jax.random.truncated_normal(key, -4.0, 4.0, (DOCS, WINDOW, RELW), jnp.float32)


def draw_teacher_query(key, part):
    key = jax.random.fold_in(key, 1)
    return drawn_field(key).astype(jnp.bfloat16)


def draw_teacher_key(key, part):
    key = jax.random.fold_in(key, 2)
    return drawn_field(key).astype(jnp.bfloat16)


def draw_student_query(key, part):
    key = jax.random.fold_in(key, 3)
    return drawn_field(key).astype(jnp.bfloat16)


def draw_student_key(key, part):
    key = jax.random.fold_in(key, 4)
    return drawn_field(key).astype(jnp.bfloat16)


def profile(amount, total, reach, slope):
    loads = [(1 << 20) // math.isqrt(rank ** slope) + 1 for rank in range(2, amount + 1)]
    surplus, holding = total - reach - (amount - 1), [1] * (amount - 1)
    while surplus > 0:
        candidates = [i for i in range(amount - 1) if holding[i] < reach]
        mass, remaining = sum([loads[i] for i in candidates]), surplus
        for i in candidates:
            more = min(reach - holding[i], max(1, remaining * loads[i] // mass), surplus)
            holding[i] = holding[i] + more
            surplus = surplus - more
    return np.array([reach] + holding)


def ragged(stream_key, count, total, bound, lean):
    if count == 2:
        one = jax.random.randint(stream_key, (), max(1, total - bound), min(bound, total - 1) + 1)
        return jnp.stack([one, total - one])
    tallies = jnp.asarray(profile(count, total, bound, lean), jnp.int32)
    twos = (count - 1) // 2
    source_of, receiver = tallies[1:1 + 2 * twos:2], tallies[2:2 + 2 * twos:2]
    margin = jnp.minimum(source_of - 1, bound - receiver)
    shifted = jax.random.randint(jax.random.fold_in(stream_key, 1), (twos,), 0, 1 << 20) % (margin + 1)
    tallies = tallies.at[1:1 + 2 * twos:2].set(source_of - shifted).at[2:2 + 2 * twos:2].set(receiver + shifted)
    return tallies[jax.random.permutation(jax.random.fold_in(stream_key, 2), count)]


def setup_inputs(seed: int = 0) -> dict:
    arg_keys = jax.random.split(jax.random.key(seed), 7)
    return {
        "teacher_query": draw_teacher_query(jax.random.fold_in(arg_keys[6], 71), 0),
        "teacher_key": draw_teacher_key(jax.random.fold_in(arg_keys[6], 71), 0),
        "student_query": draw_student_query(jax.random.fold_in(arg_keys[6], 71), 0),
        "student_key": draw_student_key(jax.random.fold_in(arg_keys[6], 71), 0),
        "segment_ids": jax.vmap(lambda own: jnp.searchsorted(jnp.cumsum(ragged(own, 2 * WINDOW // MOST + 1, WINDOW, MOST, 0)), jnp.arange(WINDOW), side="right"))(jax.random.split(arg_keys[4], DOCS)).reshape((DOCS, WINDOW)).astype(jnp.int32),
        "head_weight": jnp.clip(jnp.exp(jax.random.uniform(arg_keys[5], (HEADS,), jnp.float32, math.log(100.0), math.log(400.0))), 100.0, 400.0),
    }


def row_log_totals(scores, visible):
    masked = jnp.where(visible, scores, jnp.float32(-1e+30))
    row_top = lax.optimization_barrier(jnp.max(masked, axis=-1))
    summed = lax.optimization_barrier(jnp.sum(jnp.where(visible, jnp.exp(masked - row_top[:, None]), jnp.float32(0.0)), axis=-1))
    return row_top + jnp.log(summed)

def softmax_rows(scores, log_total, visible):
    return jnp.where(visible, jnp.exp(scores - log_total[:, None]), jnp.float32(0.0))

def reference(teacher_query, teacher_key, student_query, student_key, segment_ids, head_weight):
    score_scale = 1.0 / math.sqrt(HEAD_DIM)
    span = BAND * TOK_DEV
    lead = span - TOK_DEV
    blocks = WINDOW // TOK_DEV
    query_parts = []
    key_parts = []
    for doc_index in range(DOCS):
        pad_rows = jnp.zeros((lead, RELW), jnp.bfloat16)
        teacher_pad = jnp.concatenate([pad_rows, teacher_key[doc_index]], axis=0)
        student_pad = jnp.concatenate([pad_rows, student_key[doc_index]], axis=0)
        seg_row = segment_ids[doc_index]
        seg_pad = jnp.concatenate([jnp.full((lead,), -1, jnp.int32), seg_row], axis=0)
        teacher_doc = teacher_query[doc_index]
        student_doc = student_query[doc_index]

        def block_step(key_acc, block):
            start = (block * TOK_DEV).astype(jnp.int32)
            teacher_block = lax.dynamic_slice_in_dim(teacher_doc, start, TOK_DEV, 0)
            student_block = lax.dynamic_slice_in_dim(student_doc, start, TOK_DEV, 0)
            teacher_band = lax.dynamic_slice_in_dim(teacher_pad, start, span, 0)
            student_band = lax.dynamic_slice_in_dim(student_pad, start, span, 0)
            seg_query = lax.dynamic_slice_in_dim(seg_row, start, TOK_DEV, 0)
            seg_keys = lax.dynamic_slice_in_dim(seg_pad, start, span, 0)
            query_pos = start + jnp.arange(TOK_DEV, dtype=jnp.int32)
            key_pos = start - lead + jnp.arange(span, dtype=jnp.int32)
            visible = (key_pos[None, :] <= query_pos[:, None]) & (seg_keys[None, :] == seg_query[:, None])
            query_heads = []
            key_heads = []
            for head_index in range(HEADS):
                columns = slice(head_index * HEAD_DIM, (head_index + 1) * HEAD_DIM)
                teacher_rows = teacher_block[:, columns]
                student_rows = student_block[:, columns]
                teacher_cols = teacher_band[:, columns]
                student_cols = student_band[:, columns]
                teacher_scores = jnp.dot(teacher_rows, teacher_cols.T, preferred_element_type=jnp.float32) * score_scale
                student_scores = jnp.dot(student_rows, student_cols.T, preferred_element_type=jnp.float32) * score_scale
                teacher_total = row_log_totals(teacher_scores, visible)
                student_total = row_log_totals(student_scores, visible)
                teacher_probs = softmax_rows(teacher_scores, teacher_total, visible)
                student_probs = softmax_rows(student_scores, student_total, visible)
                grad_weights = (head_weight[head_index] * (student_probs - teacher_probs)).astype(jnp.bfloat16)
                query_heads.append(jnp.dot(grad_weights, student_cols, preferred_element_type=jnp.float32) * score_scale)
                key_heads.append(jnp.dot(grad_weights.T, student_rows, preferred_element_type=jnp.float32) * score_scale)
            key_term = jnp.concatenate(key_heads, axis=1)
            existing = lax.dynamic_slice_in_dim(key_acc, start, span, 0)
            key_acc = lax.dynamic_update_slice_in_dim(key_acc, existing + key_term, start, 0)
            return (key_acc, jnp.concatenate(query_heads, axis=1))
        start_acc = jnp.zeros((WINDOW + lead, RELW), jnp.float32)
        key_acc, query_blocks = lax.scan(block_step, start_acc, jnp.arange(blocks, dtype=jnp.int32))
        query_parts.append(query_blocks.reshape(WINDOW, RELW))
        key_parts.append(key_acc[lead:])
    query_grad = jnp.stack(query_parts, axis=0)
    key_grad = jnp.stack(key_parts, axis=0)
    return (query_grad, key_grad)
```

```python
import functools
import math

import jax
import jax.numpy as jnp
from jax import lax
from jax.experimental import pallas as pl
from jax.experimental.pallas import tpu as pltpu
from jax.sharding import PartitionSpec as P

HEADS = 4
DIM = 128
TOK = 256
ROW = 8
QUART = 4
MASKED = -1e30
F32 = jnp.float32
BF16 = jnp.bfloat16
VMEM = pl.BlockSpec(memory_space=pltpu.VMEM)
SMEM = pl.BlockSpec(memory_space=pltpu.SMEM)
AXES = ("seq", "dp")


def routes(seq, dp):
    def index(y, rest, x_lo, core):
        return ((rest * ROW + y) * (dp // 2) + x_lo) * 2 + core

    rounds = [[] for _ in range(HEADS)]
    swap, down = [], []
    for rest in range(seq // ROW):
        for y in range(ROW):
            for x_lo in range(dp // 2):
                for core in range(2):
                    me = index(y, rest, x_lo, core)
                    swap.append((me, index(y, rest, x_lo, 1 - core)))
                    if rest + 1 < seq // ROW:
                        down.append((me, index(y, rest + 1, x_lo, core)))
                    for k in range(HEADS):
                        head = (y // 2 + k) % HEADS
                        rounds[k].append((me, index(2 * head + core, rest, x_lo, y % 2)))
    return rounds, swap, down


def reverse(route):
    return [(b, a) for a, b in route]


def pack_kernel(half_ref, a_ref, b_ref, *outs):
    for k, out in enumerate(outs):
        head = lax.rem(half_ref[0] + k, HEADS)
        columns = pl.ds(pl.multiple_of(head * DIM, DIM), DIM)
        out[0] = a_ref[:, columns]
        out[1] = b_ref[:, columns]


def pack(half, a, b):
    return pl.pallas_call(
        pack_kernel,
        out_shape=[jax.ShapeDtypeStruct((2, TOK, DIM), BF16)] * HEADS,
        in_specs=[SMEM, VMEM, VMEM],
        out_specs=[VMEM] * HEADS,
        cost_estimate=pl.CostEstimate(flops=0, bytes_accessed=4 * TOK * 512 * 2, transcendentals=0),
    )(half, a, b)


def unpack_kernel(half_ref, *refs):
    out = refs[-1]
    for k in range(HEADS):
        head = lax.rem(half_ref[0] + k, HEADS)
        columns = pl.ds(pl.multiple_of(head * DIM, DIM), DIM)
        out[:, columns] = refs[k][...].astype(F32)


def unpack(half, pieces):
    return pl.pallas_call(
        unpack_kernel,
        out_shape=jax.ShapeDtypeStruct((TOK, HEADS * DIM), F32),
        in_specs=[SMEM] + [VMEM] * HEADS,
        out_specs=VMEM,
        cost_estimate=pl.CostEstimate(flops=0, bytes_accessed=6 * TOK * 512, transcendentals=0),
    )(half, *pieces)


def main_kernel(
    info_ref, low_ref, weight_ref, segq_ref, segk_ref, q0, q1, q2, q3, own_ref, oth_ref, own_prev_ref, oth_prev_ref,
    dq_ref, keep_ref, send_ref,
    kt, ks, dk, pt, ps, top_t, top_s, sum_t, sum_s, dq_acc,
):
    head, side = info_ref[0], info_ref[1]
    weight = weight_ref[0]
    scale = 1.0 / math.sqrt(DIM)
    pace = scale * math.log2(math.e)
    queries = (q0, q1, q2, q3)

    def rows(block):
        return pl.ds(pl.multiple_of(block * TOK, TOK), TOK)

    def place(k, parity):
        return 2 * lax.rem(head - k + HEADS, HEADS) + parity

    for k in range(HEADS):
        for row, (mine, theirs) in enumerate(((own_prev_ref, oth_prev_ref), (own_ref, oth_ref))):
            here, there = rows(row * ROW + place(k, side)), rows(row * ROW + place(k, 1 - side))
            kt[here, :] = mine[k, 0]
            ks[here, :] = mine[k, 1]
            kt[there, :] = theirs[k, 0]
            ks[there, :] = theirs[k, 1]

    def clear(block, _):
        dk[rows(block), :] = jnp.zeros((TOK, DIM), F32)
        return 0

    lax.fori_loop(0, 2 * ROW, clear, 0)

    def halves(op, wide):
        return op(wide[:, :DIM], wide[:, DIM:])

    for k in range(HEADS):
        here = place(k, side)
        block = ROW + here
        low = low_ref[block]
        q_t, q_s = queries[k][0], queries[k][1]
        seg_q = segq_ref[rows(here), :]

        top_t[...] = jnp.full((TOK, DIM), MASKED, F32)
        top_s[...] = jnp.full((TOK, DIM), MASKED, F32)

        def scores(kb, visible):
            dims = (((1,), (1,)), ((), ()))
            s_t = lax.dot_general(q_t, kt[rows(kb), :], dims, preferred_element_type=F32)
            s_s = lax.dot_general(q_s, ks[rows(kb), :], dims, preferred_element_type=F32)
            s_t = jnp.where(visible, s_t, MASKED)
            s_s = jnp.where(visible, s_s, MASKED)
            pt[kb - low] = s_t
            ps[kb - low] = s_s
            top_t[...] = jnp.maximum(top_t[...], halves(jnp.maximum, s_t))
            top_s[...] = jnp.maximum(top_s[...], halves(jnp.maximum, s_s))

        def first(kb, _):
            scores(kb, segk_ref[pl.ds(kb, 1), :] == seg_q)
            return 0

        lax.fori_loop(low, block, first, 0)
        causal = lax.broadcasted_iota(jnp.int32, (TOK, TOK), 1) <= lax.broadcasted_iota(jnp.int32, (TOK, TOK), 0)
        scores(block, causal & (segk_ref[pl.ds(block, 1), :] == seg_q))

        m_t = jnp.max(top_t[...], axis=1, keepdims=True)
        m_s = jnp.max(top_s[...], axis=1, keepdims=True)
        sum_t[...] = jnp.zeros((TOK, DIM), F32)
        sum_s[...] = jnp.zeros((TOK, DIM), F32)

        def second(slot, _):
            e_t = jnp.exp2((pt[slot] - m_t) * pace)
            e_s = jnp.exp2((ps[slot] - m_s) * pace)
            pt[slot] = e_t
            ps[slot] = e_s
            sum_t[...] += halves(jnp.add, e_t)
            sum_s[...] += halves(jnp.add, e_s)
            return 0

        lax.fori_loop(0, block + 1 - low, second, 0)
        r_t = weight / jnp.sum(sum_t[...], axis=1, keepdims=True)
        r_s = weight / jnp.sum(sum_s[...], axis=1, keepdims=True)
        dq_acc[...] = jnp.zeros((TOK, DIM), F32)

        def third(kb, _):
            grad = (ps[kb - low] * r_s - pt[kb - low] * r_t).astype(BF16)
            dq_acc[...] += jnp.dot(grad, ks[rows(kb), :], preferred_element_type=F32)
            dk[rows(kb), :] += lax.dot_general(grad, q_s, (((0,), (0,)), ((), ())), preferred_element_type=F32)
            return 0

        lax.fori_loop(low, block + 1, third, 0)
        dq_ref[k] = (dq_acc[...] * scale).astype(BF16)

    for k in range(HEADS):
        for row in range(2):
            keep_ref[row, k] = dk[rows(row * ROW + place(k, side)), :] * scale
            send_ref[row, k] = dk[rows(row * ROW + place(k, 1 - side)), :] * scale


def attend(info, low, weight, seg_q, seg_k, queries, own, oth, own_prev, oth_prev):
    return pl.pallas_call(
        main_kernel,
        out_shape=[
            jax.ShapeDtypeStruct((QUART, TOK, DIM), BF16),
            jax.ShapeDtypeStruct((2, QUART, TOK, DIM), F32),
            jax.ShapeDtypeStruct((2, QUART, TOK, DIM), F32),
        ],
        in_specs=[SMEM] * 3 + [VMEM] * 10,
        out_specs=[VMEM] * 3,
        scratch_shapes=[
            pltpu.VMEM((2 * ROW * TOK, DIM), BF16),
            pltpu.VMEM((2 * ROW * TOK, DIM), BF16),
            pltpu.VMEM((2 * ROW * TOK, DIM), F32),
            pltpu.VMEM((ROW, TOK, TOK), F32),
            pltpu.VMEM((ROW, TOK, TOK), F32),
            pltpu.VMEM((TOK, DIM), F32),
            pltpu.VMEM((TOK, DIM), F32),
            pltpu.VMEM((TOK, DIM), F32),
            pltpu.VMEM((TOK, DIM), F32),
            pltpu.VMEM((TOK, DIM), F32),
        ],
        compiler_params=pltpu.CompilerParams(vmem_limit_bytes=36 * 1024 * 1024),
        cost_estimate=pl.CostEstimate(flops=10**9, bytes_accessed=8 * 2**20, transcendentals=4 * 10**6),
    )(info, low, weight, seg_q, seg_k, *queries, own, oth, own_prev, oth_prev)


def per_device(seq, dp, teacher_query, teacher_key, student_query, student_key, segment_ids, head_weight):
    rounds, swap, down = routes(seq, dp)
    seq_index = lax.axis_index("seq")
    core = lax.rem(lax.axis_index("dp"), 2)
    y = lax.rem(seq_index, ROW)
    row_index = seq_index // ROW
    head, window = y // 2, lax.rem(y, 2)
    half = head.reshape(1)

    def move(x, route):
        return lax.ppermute(x, AXES, route)

    keys = [move(x, r) for x, r in zip(pack(half, teacher_key[0], student_key[0]), rounds)]
    queries = [move(x, r) for x, r in zip(pack(half, teacher_query[0], student_query[0]), rounds)]

    row_tokens = ROW * TOK
    filler = jnp.full((row_tokens,), -1, jnp.int32)
    seg_mine = lax.dynamic_slice_in_dim(
        jnp.concatenate([filler, segment_ids[0]]), row_index * row_tokens, 2 * row_tokens
    ).reshape(2 * ROW, TOK)
    seg = jnp.where(core == window, seg_mine, move(seg_mine, swap))
    reach = (seg[None, :, TOK - 1] == seg[:, None, 0]) & (
        jnp.arange(2 * ROW)[None, :] < jnp.arange(2 * ROW)[:, None]
    )
    low = jnp.arange(2 * ROW, dtype=jnp.int32) - jnp.sum(reach, axis=1, dtype=jnp.int32)
    seg_q = seg[ROW:].reshape(row_tokens, 1)

    own = jnp.stack(keys)
    own_prev = move(own, down)
    oth = move(own, swap)
    oth_prev = move(own_prev, swap)

    info = jnp.stack([head, core]).astype(jnp.int32)
    weight = lax.dynamic_slice_in_dim(head_weight, head, 1)
    dq, keep, send = attend(info, low, weight, seg_q, seg, queries, own, oth, own_prev, oth_prev)

    query_grad = unpack(half, [move(dq[k], reverse(rounds[k])) for k in range(HEADS)])

    both = keep + move(send, swap)
    back = move(both[0].astype(BF16), reverse(down))
    total = (both[1] + back.astype(F32)).astype(BF16)
    key_grad = unpack(half, [move(total[k], reverse(rounds[k])) for k in range(HEADS)])
    return query_grad[None], key_grad[None]


def solution(mesh):
    seq, dp = mesh.shape["seq"], mesh.shape["dp"]
    spec = P("dp", "seq", None)
    return jax.shard_map(
        functools.partial(per_device, seq, dp),
        mesh=mesh,
        in_specs=(spec, spec, spec, spec, P("dp", None), P()),
        out_specs=(spec, spec),
        check_vma=False,
    )
```

```python
import functools
import math

import jax
import jax.numpy as jnp
from jax import lax
from jax.experimental import pallas as pl
from jax.experimental.pallas import tpu as pltpu
from jax.sharding import PartitionSpec as P

HEADS = 4
DIM = 128
TOK = 256
ROW = 8
QUART = 4
MASKED = -1e30
F32 = jnp.float32
BF16 = jnp.bfloat16
VMEM = pl.BlockSpec(memory_space=pltpu.VMEM)
SMEM = pl.BlockSpec(memory_space=pltpu.SMEM)
AXES = ("seq", "dp")


def routes(seq, dp):
    def index(y, rest, x_lo, core):
        return ((rest * ROW + y) * (dp // 2) + x_lo) * 2 + core

    rounds = [[] for _ in range(HEADS)]
    swap, down = [], []
    for rest in range(seq // ROW):
        for y in range(ROW):
            for x_lo in range(dp // 2):
                for core in range(2):
                    me = index(y, rest, x_lo, core)
                    swap.append((me, index(y, rest, x_lo, 1 - core)))
                    if rest + 1 < seq // ROW:
                        down.append((me, index(y, rest + 1, x_lo, core)))
                    for k in range(HEADS):
                        head = (y // 2 + k) % HEADS
                        rounds[k].append((me, index(2 * head + core, rest, x_lo, y % 2)))
    return rounds, swap, down


def reverse(route):
    return [(b, a) for a, b in route]


def pack_kernel(half_ref, a_ref, b_ref, c_ref, d_ref, *outs):
    for k, out in enumerate(outs):
        head = lax.rem(half_ref[0] + k, HEADS)
        columns = pl.ds(pl.multiple_of(head * DIM, DIM), DIM)
        for i, ref in enumerate((a_ref, b_ref, c_ref, d_ref)):
            out[i] = ref[:, columns]


def pack(half, *states):
    return pl.pallas_call(
        pack_kernel,
        out_shape=[jax.ShapeDtypeStruct((4, TOK, DIM), BF16)] * HEADS,
        in_specs=[SMEM] + [VMEM] * 4,
        out_specs=[VMEM] * HEADS,
        cost_estimate=pl.CostEstimate(flops=0, bytes_accessed=8 * TOK * 512 * 2, transcendentals=0),
    )(half, *states)


def unpack_kernel(half_ref, p0, p1, p2, p3, query_ref, key_ref):
    for k, piece in enumerate((p0, p1, p2, p3)):
        head = lax.rem(half_ref[0] + k, HEADS)
        columns = pl.ds(pl.multiple_of(head * DIM, DIM), DIM)
        query_ref[:, columns] = piece[0].astype(F32)
        key_ref[:, columns] = piece[1].astype(F32)


def unpack(half, pieces):
    return pl.pallas_call(
        unpack_kernel,
        out_shape=[jax.ShapeDtypeStruct((TOK, HEADS * DIM), F32)] * 2,
        in_specs=[SMEM] + [VMEM] * HEADS,
        out_specs=[VMEM] * 2,
        cost_estimate=pl.CostEstimate(flops=0, bytes_accessed=12 * TOK * 512, transcendentals=0),
    )(half, *pieces)


def finish_kernel(dq_ref, keep_ref, recv_ref, back_ref, *outs):
    for k, out in enumerate(outs):
        out[0] = dq_ref[k]
        out[1] = (keep_ref[1, k] + recv_ref[1, k] + back_ref[k].astype(F32)).astype(BF16)


def finish(dq, keep, recv, back):
    return pl.pallas_call(
        finish_kernel,
        out_shape=[jax.ShapeDtypeStruct((2, TOK, DIM), BF16)] * HEADS,
        in_specs=[VMEM] * 4,
        out_specs=[VMEM] * HEADS,
        cost_estimate=pl.CostEstimate(flops=0, bytes_accessed=4 * 2**20, transcendentals=0),
    )(dq, keep, recv, back)


def main_kernel(
    info_ref, low_ref, weight_ref, start_ref, p0, p1, p2, p3, oth_ref, own_prev_ref, oth_prev_ref,
    dq_ref, keep_ref, send_ref,
    kt, ks, ks_turned, dk, et, es, top_t, top_s, dq_acc,
):
    head, side = info_ref[0], info_ref[1]
    weight = weight_ref[0]
    scale = 1.0 / math.sqrt(DIM)
    pace = scale * math.log2(math.e)
    pieces = (p0, p1, p2, p3)
    along_depth = (((1,), (1,)), ((), ()))

    def rows(block):
        return pl.ds(pl.multiple_of(block * TOK, TOK), TOK)

    def place(k, parity):
        return 2 * lax.rem(head - k + HEADS, HEADS) + parity

    for k in range(HEADS):
        blocks = (
            (place(k, side), own_prev_ref.at[k]),
            (place(k, 1 - side), oth_prev_ref.at[k]),
            (ROW + place(k, side), pieces[k]),
            (ROW + place(k, 1 - side), oth_ref.at[k]),
        )
        for block, ref in blocks:
            kt[rows(block), :] = ref[0]
            ks[rows(block), :] = ref[1]

    def prepare(block, _):
        ks_turned[block] = ks[rows(block), :].T
        dk[rows(block), :] = jnp.zeros((TOK, DIM), F32)
        return 0

    lax.fori_loop(0, 2 * ROW, prepare, 0)

    key_row = lax.broadcasted_iota(jnp.int32, (TOK, TOK), 0)
    query_column = lax.broadcasted_iota(jnp.int32, (TOK, TOK), 1)

    for k in range(HEADS):
        here = place(k, side)
        block = ROW + here
        low = low_ref[here] // TOK
        q_t, q_s = pieces[k][2], pieces[k][3]
        start = start_ref[pl.ds(here, 1), :]

        def one(keys, queries, visible, slot, top, total, top_out, out):
            s = lax.dot_general(keys, queries, along_depth, preferred_element_type=F32)
            s = jnp.where(visible, s, MASKED)
            new_top = jnp.maximum(top, jnp.max(s, axis=0, keepdims=True))
            e = jnp.exp2((s - new_top) * pace)
            out[slot] = e
            top_out[slot] = new_top
            return new_top, total * jnp.exp2((top - new_top) * pace) + jnp.sum(e, axis=0, keepdims=True)

        def score(kb, visible, carry):
            m_t, l_t, m_s, l_s = carry
            m_t, l_t = one(kt[rows(kb), :], q_t, visible, kb - low, m_t, l_t, top_t, et)
            m_s, l_s = one(ks[rows(kb), :], q_s, visible, kb - low, m_s, l_s, top_s, es)
            return m_t, l_t, m_s, l_s

        def score_before(kb, carry):
            return score(kb, key_row >= start - kb * TOK, carry)

        none, zero = jnp.full((1, TOK), MASKED, F32), jnp.zeros((1, TOK), F32)
        own_visible = (key_row <= query_column) & (key_row >= start - block * TOK)
        carry = score(block, own_visible, (none, zero, none, zero))
        m_t, l_t, m_s, l_s = lax.fori_loop(low, block, score_before, carry)
        r_t, r_s = weight / l_t, weight / l_s
        dq_acc[...] = jnp.zeros((DIM, TOK), F32)

        def grads(kb, _):
            slot = kb - low
            f_t = jnp.exp2((top_t[slot] - m_t) * pace) * r_t
            f_s = jnp.exp2((top_s[slot] - m_s) * pace) * r_s
            grad = (es[slot] * f_s - et[slot] * f_t).astype(BF16)
            dk[rows(kb), :] += jnp.dot(grad, q_s, preferred_element_type=F32)
            dq_acc[...] += jnp.dot(ks_turned[kb], grad, preferred_element_type=F32)
            return 0

        lax.fori_loop(low, block + 1, grads, 0)
        dq_ref[k] = (dq_acc[...] * scale).T.astype(BF16)

    for k in range(HEADS):
        for row in range(2):
            keep_ref[row, k] = dk[rows(row * ROW + place(k, side)), :] * scale
            send_ref[row, k] = dk[rows(row * ROW + place(k, 1 - side)), :] * scale


def attend(info, low, weight, start, pieces, oth, own_prev, oth_prev):
    return pl.pallas_call(
        main_kernel,
        out_shape=[
            jax.ShapeDtypeStruct((QUART, TOK, DIM), BF16),
            jax.ShapeDtypeStruct((2, QUART, TOK, DIM), F32),
            jax.ShapeDtypeStruct((2, QUART, TOK, DIM), F32),
        ],
        in_specs=[SMEM] * 3 + [VMEM] * 8,
        out_specs=[VMEM] * 3,
        scratch_shapes=[
            pltpu.VMEM((2 * ROW * TOK, DIM), BF16),
            pltpu.VMEM((2 * ROW * TOK, DIM), BF16),
            pltpu.VMEM((2 * ROW, DIM, TOK), BF16),
            pltpu.VMEM((2 * ROW * TOK, DIM), F32),
            pltpu.VMEM((ROW, TOK, TOK), F32),
            pltpu.VMEM((ROW, TOK, TOK), F32),
            pltpu.VMEM((ROW, 1, TOK), F32),
            pltpu.VMEM((ROW, 1, TOK), F32),
            pltpu.VMEM((DIM, TOK), F32),
        ],
        compiler_params=pltpu.CompilerParams(vmem_limit_bytes=36 * 1024 * 1024),
        cost_estimate=pl.CostEstimate(flops=10**9, bytes_accessed=8 * 2**20, transcendentals=4 * 10**6),
    )(info, low, weight, start, *pieces, oth, own_prev, oth_prev)


def per_device(seq, dp, teacher_query, teacher_key, student_query, student_key, segment_ids, head_weight):
    rounds, swap, down = routes(seq, dp)
    seq_index = lax.axis_index("seq")
    core = lax.rem(lax.axis_index("dp"), 2)
    y = lax.rem(seq_index, ROW)
    row_index = seq_index // ROW
    head, window = y // 2, lax.rem(y, 2)
    half = head.reshape(1)

    def move(x, route):
        return lax.ppermute(x, AXES, route)

    packed = pack(half, teacher_key[0], student_key[0], teacher_query[0], student_query[0])
    pieces = [move(x, r) for x, r in zip(packed, rounds)]

    row_tokens = ROW * TOK
    filler = jnp.full((row_tokens,), -1, jnp.int32)
    seg_mine = lax.dynamic_slice_in_dim(
        jnp.concatenate([filler, segment_ids[0]]), row_index * row_tokens, 2 * row_tokens
    ).reshape(2 * ROW, TOK)
    seg = jnp.where(core == window, seg_mine, move(seg_mine, swap))
    start = jnp.sum(
        seg.reshape(2 * row_tokens, 1, 1) < seg[None, ROW:], axis=0, dtype=jnp.int32
    )

    own = jnp.stack([piece[:2] for piece in pieces])
    own_prev = move(own, down)
    oth = move(own, swap)
    oth_prev = move(own_prev, swap)

    info = jnp.stack([head, core]).astype(jnp.int32)
    weight = lax.dynamic_slice_in_dim(head_weight, head, 1)
    dq, keep, send = attend(info, start[:, 0], weight, start, pieces, oth, own_prev, oth_prev)

    recv = move(send, swap)
    back = move((keep[0] + recv[0]).astype(BF16), reverse(down))
    results = finish(dq, keep, recv, back)
    query_grad, key_grad = unpack(half, [move(x, reverse(r)) for x, r in zip(results, rounds)])
    return query_grad[None], key_grad[None]


def solution(mesh):
    seq, dp = mesh.shape["seq"], mesh.shape["dp"]
    spec = P("dp", "seq", None)
    return jax.shard_map(
        functools.partial(per_device, seq, dp),
        mesh=mesh,
        in_specs=(spec, spec, spec, spec, P("dp", None), P()),
        out_specs=(spec, spec),
        check_vma=False,
    )
```

```python
import functools
import math

import jax
import jax.numpy as jnp
from jax import lax
from jax.experimental import pallas as pl
from jax.experimental.pallas import tpu as pltpu
from jax.sharding import PartitionSpec as P

HEADS = 4
DIM = 128
TOK = 256
LINE = 4
RING = 8
BEHIND = 7
BAND = 12
OWN = 8
PAIR = 2 * TOK
MASKED = -1e30
F32 = jnp.float32
BF16 = jnp.bfloat16
VMEM = pl.BlockSpec(memory_space=pltpu.VMEM)
SMEM = pl.BlockSpec(memory_space=pltpu.SMEM)
AXES = ("seq", "dp")


def routes(seq, dp):
    last, before_last = [], []
    for ring in range(seq // RING):
        for y in range(RING):
            for part in range(dp):
                me = (ring * RING + y) * dp + part
                ahead = ring + (y >= LINE)
                if ahead < seq // RING:
                    last.append((me, (ahead * RING + RING - 1 - y) * dp + part))
                if ring + 1 < seq // RING:
                    before_last.append((me, ((ring + 1) * RING + y) * dp + part))
    return last, before_last


def reverse(route):
    return [(b, a) for a, b in route]


def head_columns(flip, place):
    head = jnp.where(flip == 1, HEADS - 1 - place, place)
    return pl.ds(pl.multiple_of(head * DIM, DIM), DIM)


def pack_keys_kernel(flip_ref, a_ref, b_ref, out_ref):
    for place in range(HEADS):
        columns = head_columns(flip_ref[0], place)
        out_ref[place, 0] = a_ref[:, columns]
        out_ref[place, 1] = b_ref[:, columns]


def pack_queries_kernel(flip_ref, range_ref, a_ref, b_ref, seg_ref, out_ref, start_ref, low_ref):
    pack_keys_kernel(flip_ref, a_ref, b_ref, out_ref)
    first_block = range_ref[0] * LINE

    def ids(block):
        return seg_ref[0:1, pl.ds(pl.multiple_of(block * TOK, TOK), TOK)]

    own = [ids(first_block + j) for j in range(LINE)]
    ahead = [(first_block - b, ids(jnp.maximum(first_block - b, 0))) for b in range(1, BEHIND + 1)]
    counts = []
    for j in range(LINE):
        first = own[j][:, :1]
        same = jnp.zeros((1, TOK), jnp.int32)
        for i in range(j):
            same += (own[i] == first).astype(jnp.int32)
        for block, row in ahead[: BEHIND - j]:
            same += ((row == first) & (block >= 0)).astype(jnp.int32)
        counts.append(same)
    count = jnp.sum(jnp.concatenate(counts, axis=0), axis=1, keepdims=True)
    seg = jnp.concatenate(own, axis=0)
    column = lax.broadcasted_iota(jnp.int32, (LINE, TOK), 1)
    begin = jnp.where(seg != pltpu.roll(seg, 1, 1), column, 0)
    begin = jnp.where(column == 0, 0, begin)
    step = 1
    while step < TOK:
        begin = jnp.maximum(begin, jnp.where(column >= step, pltpu.roll(begin, step, 1), 0))
        step *= 2
    block_at = (OWN + lax.broadcasted_iota(jnp.int32, (LINE, TOK), 0)) * TOK
    start = block_at + jnp.where(begin > 0, begin, -count)
    start_ref[...] = start
    for j in range(LINE):
        low_ref[j] = jnp.min(start[j : j + 1, :])


def pack_keys(flip, a, b):
    return pl.pallas_call(
        pack_keys_kernel,
        out_shape=jax.ShapeDtypeStruct((HEADS, 2, TOK, DIM), BF16),
        in_specs=[SMEM, VMEM, VMEM],
        out_specs=VMEM,
        cost_estimate=pl.CostEstimate(flops=0, bytes_accessed=2**20, transcendentals=0),
    )(flip, a, b)


def pack_queries(flip, range_index, a, b, seg):
    return pl.pallas_call(
        pack_queries_kernel,
        out_shape=[
            jax.ShapeDtypeStruct((HEADS, 2, TOK, DIM), BF16),
            jax.ShapeDtypeStruct((LINE, TOK), jnp.int32),
            jax.ShapeDtypeStruct((LINE,), jnp.int32),
        ],
        in_specs=[SMEM, SMEM, VMEM, VMEM, VMEM],
        out_specs=[VMEM, VMEM, SMEM],
        cost_estimate=pl.CostEstimate(flops=0, bytes_accessed=2**20, transcendentals=0),
    )(flip, range_index, a, b, seg)


def unpack_kernel(flip_ref, dq_ref, dk_ref, query_ref, key_ref):
    for place in range(HEADS):
        columns = head_columns(flip_ref[0], place)
        query_ref[:, columns] = dq_ref[place].astype(F32)
        key_ref[:, columns] = dk_ref[place].astype(F32)


def unpack(flip, dq, dk):
    return pl.pallas_call(
        unpack_kernel,
        out_shape=[jax.ShapeDtypeStruct((TOK, HEADS * DIM), F32)] * 2,
        in_specs=[SMEM, VMEM, VMEM],
        out_specs=[VMEM] * 2,
        cost_estimate=pl.CostEstimate(flops=0, bytes_accessed=12 * TOK * 512, transcendentals=0),
    )(flip, dq, dk)


def main_kernel(
    head_ref, low_ref, weight_ref, start_ref, query_ref, own_ref, last_ref, before_ref,
    dq_ref, dk_own_ref, dk_last_ref, dk_before_ref,
    kt, ks, ks_turned, dk, et, es, top_t, top_s, dq_acc,
):
    weight = weight_ref[head_ref[0]]
    scale = 1.0 / math.sqrt(DIM)
    pace = scale * math.log2(math.e)
    along_depth = (((1,), (1,)), ((), ()))
    lowest = low_ref[0] // TOK

    def rows(block):
        return pl.ds(block * TOK, TOK)

    def load(block, ref, index):
        kt[rows(block), :] = ref[index, 0]
        ks[rows(block), :] = ref[index, 1]
        ks_turned[:, rows(block)] = ref[index, 1].T
        dk[rows(block), :] = jnp.zeros((TOK, DIM), F32)

    def clear(block):
        kt[rows(block), :] = jnp.zeros((TOK, DIM), BF16)
        ks[rows(block), :] = jnp.zeros((TOK, DIM), BF16)
        ks_turned[:, rows(block)] = jnp.zeros((DIM, TOK), BF16)
        dk[rows(block), :] = jnp.zeros((TOK, DIM), F32)

    for i in range(LINE):
        load(OWN + i, own_ref, i)

    @pl.when(lowest <= OWN)
    def _():
        for i in range(LINE):
            load(LINE + i, last_ref, i)

    @pl.when(lowest > OWN)
    def _():
        for i in range(LINE):
            clear(LINE + i)

    @pl.when(lowest <= LINE)
    def _():
        for i in range(LINE - 1):
            load(1 + i, before_ref, i)

    @pl.when(lowest > LINE)
    def _():
        for i in range(LINE - 1):
            clear(1 + i)

    key_row = lax.broadcasted_iota(jnp.int32, (PAIR, TOK), 0)
    query_column = lax.broadcasted_iota(jnp.int32, (PAIR, TOK), 1)

    for j in range(LINE):
        block = OWN + j
        pairs = (block + 2 - low_ref[j] // TOK) // 2
        q_t, q_s = query_ref[j, 0], query_ref[j, 1]
        start = start_ref[j : j + 1, :]

        def at(t):
            return pl.multiple_of((block - 1 - 2 * t) * TOK, TOK)

        def one(keys, queries, visible, t, top, total, top_out, out):
            s = lax.dot_general(keys, queries, along_depth, preferred_element_type=F32)
            s = jnp.where(visible, s, MASKED)
            new_top = jnp.maximum(top, jnp.max(s, axis=0, keepdims=True))
            e = jnp.exp2((s - new_top) * pace)
            out[t] = e
            top_out[t] = new_top
            return new_top, total * jnp.exp2((top - new_top) * pace) + jnp.sum(e, axis=0, keepdims=True)

        def score(t, visible, carry):
            m_t, l_t, m_s, l_s = carry
            here = pl.ds(at(t), PAIR)
            m_t, l_t = one(kt[here, :], q_t, visible, t, m_t, l_t, top_t, et)
            m_s, l_s = one(ks[here, :], q_s, visible, t, m_s, l_s, top_s, es)
            return m_t, l_t, m_s, l_s

        def score_before(t, carry):
            return score(t, key_row >= start - at(t), carry)

        none, zero = jnp.full((1, TOK), MASKED, F32), jnp.zeros((1, TOK), F32)
        own_visible = (key_row <= query_column + TOK) & (key_row >= start - at(0))
        carry = score(0, own_visible, (none, zero, none, zero))
        m_t, l_t, m_s, l_s = lax.fori_loop(1, pairs, score_before, carry)
        r_t, r_s = weight / l_t, weight / l_s
        dq_acc[...] = jnp.zeros((DIM, TOK), F32)

        def grads(t, _):
            here = pl.ds(at(t), PAIR)
            f_t = jnp.exp2((top_t[t] - m_t) * pace) * r_t
            f_s = jnp.exp2((top_s[t] - m_s) * pace) * r_s
            grad = (es[t] * f_s - et[t] * f_t).astype(BF16)
            dk[here, :] += jnp.dot(grad, q_s, preferred_element_type=F32)
            dq_acc[...] += jnp.dot(ks_turned[:, here], grad, preferred_element_type=F32)
            return 0

        lax.fori_loop(0, pairs, grads, 0)
        dq_ref[j] = (dq_acc[...] * scale).T.astype(BF16)

    for i in range(LINE):
        dk_own_ref[i] = dk[rows(OWN + i), :] * scale
        dk_last_ref[i] = (dk[rows(LINE + i), :] * scale).astype(BF16)
    for i in range(LINE - 1):
        dk_before_ref[i] = (dk[rows(1 + i), :] * scale).astype(BF16)


def attend(head, low, weight, start, queries, own, last, before):
    return pl.pallas_call(
        main_kernel,
        out_shape=[
            jax.ShapeDtypeStruct((LINE, TOK, DIM), BF16),
            jax.ShapeDtypeStruct((LINE, TOK, DIM), F32),
            jax.ShapeDtypeStruct((LINE, TOK, DIM), BF16),
            jax.ShapeDtypeStruct((LINE - 1, TOK, DIM), BF16),
        ],
        in_specs=[SMEM] * 3 + [VMEM] * 5,
        out_specs=[VMEM] * 4,
        scratch_shapes=[
            pltpu.VMEM((BAND * TOK, DIM), BF16),
            pltpu.VMEM((BAND * TOK, DIM), BF16),
            pltpu.VMEM((DIM, BAND * TOK), BF16),
            pltpu.VMEM((BAND * TOK, DIM), F32),
            pltpu.VMEM((LINE, PAIR, TOK), F32),
            pltpu.VMEM((LINE, PAIR, TOK), F32),
            pltpu.VMEM((LINE, 1, TOK), F32),
            pltpu.VMEM((LINE, 1, TOK), F32),
            pltpu.VMEM((DIM, TOK), F32),
        ],
        compiler_params=pltpu.CompilerParams(vmem_limit_bytes=32 * 1024 * 1024),
        cost_estimate=pl.CostEstimate(flops=10**9, bytes_accessed=6 * 2**20, transcendentals=4 * 10**6),
    )(head, low, weight, start, queries, own, last, before)


def per_device(seq, dp, teacher_query, teacher_key, student_query, student_key, segment_ids, head_weight):
    to_next, to_second = routes(seq, dp)
    lines = [list(range(i, i + LINE)) for i in range(0, seq, LINE)]
    seq_index = lax.axis_index("seq")
    range_index = seq_index // LINE
    flip = lax.rem(range_index, 2)
    place = lax.rem(seq_index, LINE)
    head = jnp.where(flip == 1, HEADS - 1 - place, place)

    def move(x, route):
        return lax.ppermute(x, AXES, route)

    def exchange(x):
        return lax.all_to_all(x, "seq", 0, 0, axis_index_groups=lines)

    flip, range_index, head = flip.reshape(1), range_index.reshape(1), head.reshape(1)
    own = exchange(pack_keys(flip, teacher_key[0], student_key[0]))
    last = move(own, to_next)
    before = move(own[1:], to_second)
    packed, start, low = pack_queries(flip, range_index, teacher_query[0], student_query[0], segment_ids)
    queries = exchange(packed)
    dq, dk_own, dk_last, dk_before = attend(head, low, head_weight, start, queries, own, last, before)

    back_last = move(dk_last, reverse(to_next)).astype(F32)
    back_before = move(dk_before, reverse(to_second)).astype(F32)
    dq_home = exchange(dq)
    total = dk_own + back_last + jnp.pad(back_before, ((1, 0), (0, 0), (0, 0)))
    query_grad, key_grad = unpack(flip, dq_home, exchange(total.astype(BF16)))
    return query_grad[None], key_grad[None]


def solution(mesh):
    seq, dp = mesh.shape["seq"], mesh.shape["dp"]
    spec = P("dp", "seq", None)
    return jax.shard_map(
        functools.partial(per_device, seq, dp),
        mesh=mesh,
        in_specs=(spec, spec, spec, spec, P("dp", None), P()),
        out_specs=(spec, spec),
        check_vma=False,
    )
```

```python
import functools
import math

import jax
import jax.numpy as jnp
from jax import lax
from jax.experimental import pallas as pl
from jax.experimental.pallas import tpu as pltpu
from jax.sharding import PartitionSpec as P

HEADS = 4
DIM = 128
TOK = 256
LINE = 4
RING = 8
BEHIND = 7
BAND = 12
OWN = 8
PAIR = 2 * TOK
MASKED = -1e30
F32 = jnp.float32
BF16 = jnp.bfloat16
VMEM = pl.BlockSpec(memory_space=pltpu.VMEM)
SMEM = pl.BlockSpec(memory_space=pltpu.SMEM)
AXES = ("seq", "dp")


def routes(seq, dp):
    last, before_last = [], []
    for ring in range(seq // RING):
        for y in range(RING):
            for part in range(dp):
                me = (ring * RING + y) * dp + part
                ahead = ring + (y >= LINE)
                if ahead < seq // RING:
                    last.append((me, (ahead * RING + RING - 1 - y) * dp + part))
                if ring + 1 < seq // RING:
                    before_last.append((me, ((ring + 1) * RING + y) * dp + part))
    return last, before_last


def reverse(route):
    return [(b, a) for a, b in route]


def head_columns(flip, place):
    head = jnp.where(flip == 1, HEADS - 1 - place, place)
    return pl.ds(pl.multiple_of(head * DIM, DIM), DIM)


def pack_keys_kernel(flip_ref, a_ref, b_ref, a_out_ref, b_out_ref):
    for place in range(HEADS):
        columns = head_columns(flip_ref[0], place)
        a_out_ref[place] = a_ref[:, columns]
        b_out_ref[place] = b_ref[:, columns]


def pack_queries_kernel(flip_ref, range_ref, a_ref, b_ref, seg_ref, out_ref, start_ref, low_ref):
    for place in range(HEADS):
        columns = head_columns(flip_ref[0], place)
        out_ref[place, 0] = a_ref[:, columns]
        out_ref[place, 1] = b_ref[:, columns]
    first_block = range_ref[0] * LINE

    def ids(block):
        return seg_ref[0:1, pl.ds(pl.multiple_of(block * TOK, TOK), TOK)]

    own = [ids(first_block + j) for j in range(LINE)]
    ahead = [(first_block - b, ids(jnp.maximum(first_block - b, 0))) for b in range(1, BEHIND + 1)]
    counts = []
    for j in range(LINE):
        first = own[j][:, :1]
        same = jnp.zeros((1, TOK), jnp.int32)
        for i in range(j):
            same += (own[i] == first).astype(jnp.int32)
        for block, row in ahead[: BEHIND - j]:
            same += ((row == first) & (block >= 0)).astype(jnp.int32)
        counts.append(same)
    count = jnp.sum(jnp.concatenate(counts, axis=0), axis=1, keepdims=True)
    seg = jnp.concatenate(own, axis=0)
    column = lax.broadcasted_iota(jnp.int32, (LINE, TOK), 1)
    begin = jnp.where(seg != pltpu.roll(seg, 1, 1), column, 0)
    begin = jnp.where(column == 0, 0, begin)
    step = 1
    while step < TOK:
        begin = jnp.maximum(begin, jnp.where(column >= step, pltpu.roll(begin, step, 1), 0))
        step *= 2
    block_at = (OWN + lax.broadcasted_iota(jnp.int32, (LINE, TOK), 0)) * TOK
    start = block_at + jnp.where(begin > 0, begin, -count)
    start_ref[...] = start
    for j in range(LINE):
        low_ref[j] = jnp.min(start[j : j + 1, :])


def pack_keys(flip, a, b):
    return pl.pallas_call(
        pack_keys_kernel,
        out_shape=[jax.ShapeDtypeStruct((HEADS, TOK, DIM), BF16)] * 2,
        in_specs=[SMEM, VMEM, VMEM],
        out_specs=[VMEM] * 2,
        cost_estimate=pl.CostEstimate(flops=0, bytes_accessed=2**20, transcendentals=0),
    )(flip, a, b)


def pack_queries(flip, range_index, a, b, seg):
    return pl.pallas_call(
        pack_queries_kernel,
        out_shape=[
            jax.ShapeDtypeStruct((HEADS, 2, TOK, DIM), BF16),
            jax.ShapeDtypeStruct((LINE, TOK), jnp.int32),
            jax.ShapeDtypeStruct((LINE,), jnp.int32),
        ],
        in_specs=[SMEM, SMEM, VMEM, VMEM, VMEM],
        out_specs=[VMEM, VMEM, SMEM],
        cost_estimate=pl.CostEstimate(flops=0, bytes_accessed=2**20, transcendentals=0),
    )(flip, range_index, a, b, seg)


def unpack_kernel(flip_ref, dq_ref, dk_ref, query_ref, key_ref):
    for place in range(HEADS):
        columns = head_columns(flip_ref[0], place)
        query_ref[:, columns] = dq_ref[place].astype(F32)
        key_ref[:, columns] = dk_ref[place].astype(F32)


def unpack(flip, dq, dk):
    return pl.pallas_call(
        unpack_kernel,
        out_shape=[jax.ShapeDtypeStruct((TOK, HEADS * DIM), F32)] * 2,
        in_specs=[SMEM, VMEM, VMEM],
        out_specs=[VMEM] * 2,
        cost_estimate=pl.CostEstimate(flops=0, bytes_accessed=12 * TOK * 512, transcendentals=0),
    )(flip, dq, dk)


def main_kernel(
    head_ref, low_ref, weight_ref, start_ref, query_ref, own_t_ref, own_s_ref, last_t_ref, last_s_ref, before_ref,
    dq_ref, dk_own_ref, dk_last_ref, dk_before_ref,
    kt, ks, ks_turned, dk, et, es, top_t, top_s, dq_acc,
):
    weight = weight_ref[head_ref[0]]
    scale = 1.0 / math.sqrt(DIM)
    pace = scale * math.log2(math.e)
    along_depth = (((1,), (1,)), ((), ()))
    lowest = low_ref[0] // TOK

    def rows(block):
        return pl.ds(block * TOK, TOK)

    def load(block, teacher, student):
        kt[rows(block), :] = teacher
        ks[rows(block), :] = student
        ks_turned[:, rows(block)] = student.T
        dk[rows(block), :] = jnp.zeros((TOK, DIM), F32)

    def clear(block):
        kt[rows(block), :] = jnp.zeros((TOK, DIM), BF16)
        ks[rows(block), :] = jnp.zeros((TOK, DIM), BF16)
        ks_turned[:, rows(block)] = jnp.zeros((DIM, TOK), BF16)
        dk[rows(block), :] = jnp.zeros((TOK, DIM), F32)

    for i in range(LINE):
        load(OWN + i, own_t_ref[i], own_s_ref[i])

    @pl.when(lowest <= OWN)
    def _():
        for i in range(LINE):
            load(LINE + i, last_t_ref[i], last_s_ref[i])

    @pl.when(lowest > OWN)
    def _():
        for i in range(LINE):
            clear(LINE + i)

    @pl.when(lowest <= LINE)
    def _():
        for i in range(LINE - 1):
            load(1 + i, before_ref[0, i], before_ref[1, i])

    @pl.when(lowest > LINE)
    def _():
        for i in range(LINE - 1):
            clear(1 + i)

    key_row = lax.broadcasted_iota(jnp.int32, (PAIR, TOK), 0)
    query_column = lax.broadcasted_iota(jnp.int32, (PAIR, TOK), 1)

    for j in range(LINE):
        block = OWN + j
        pairs = (block + 2 - low_ref[j] // TOK) // 2
        q_t, q_s = query_ref[j, 0], query_ref[j, 1]
        start = start_ref[j : j + 1, :]

        def at(t):
            return pl.multiple_of((block - 1 - 2 * t) * TOK, TOK)

        def one(keys, queries, visible, t, top, total, top_out, out):
            s = lax.dot_general(keys, queries, along_depth, preferred_element_type=F32)
            s = jnp.where(visible, s, MASKED)
            new_top = jnp.maximum(top, jnp.max(s, axis=0, keepdims=True))
            e = jnp.exp2((s - new_top) * pace)
            out[t] = e
            top_out[t] = new_top
            return new_top, total * jnp.exp2((top - new_top) * pace) + jnp.sum(e, axis=0, keepdims=True)

        def score(t, visible, carry):
            m_t, l_t, m_s, l_s = carry
            here = pl.ds(at(t), PAIR)
            m_t, l_t = one(kt[here, :], q_t, visible, t, m_t, l_t, top_t, et)
            m_s, l_s = one(ks[here, :], q_s, visible, t, m_s, l_s, top_s, es)
            return m_t, l_t, m_s, l_s

        def score_before(t, carry):
            return score(t, key_row >= start - at(t), carry)

        none, zero = jnp.full((1, TOK), MASKED, F32), jnp.zeros((1, TOK), F32)
        own_visible = (key_row <= query_column + TOK) & (key_row >= start - at(0))
        carry = score(0, own_visible, (none, zero, none, zero))
        m_t, l_t, m_s, l_s = lax.fori_loop(1, pairs, score_before, carry)
        r_t, r_s = weight / l_t, weight / l_s
        dq_acc[...] = jnp.zeros((DIM, TOK), F32)

        def grads(t, _):
            here = pl.ds(at(t), PAIR)
            f_t = jnp.exp2((top_t[t] - m_t) * pace) * r_t
            f_s = jnp.exp2((top_s[t] - m_s) * pace) * r_s
            grad = (es[t] * f_s - et[t] * f_t).astype(BF16)
            dk[here, :] += jnp.dot(grad, q_s, preferred_element_type=F32)
            dq_acc[...] += jnp.dot(ks_turned[:, here], grad, preferred_element_type=F32)
            return 0

        lax.fori_loop(0, pairs, grads, 0)
        dq_ref[j] = (dq_acc[...] * scale).T.astype(BF16)

    for i in range(LINE):
        dk_own_ref[i] = dk[rows(OWN + i), :] * scale
        dk_last_ref[i] = (dk[rows(LINE + i), :] * scale).astype(BF16)
    for i in range(LINE - 1):
        dk_before_ref[i] = (dk[rows(1 + i), :] * scale).astype(BF16)


def attend(head, low, weight, start, queries, *keys):
    return pl.pallas_call(
        main_kernel,
        out_shape=[
            jax.ShapeDtypeStruct((LINE, TOK, DIM), BF16),
            jax.ShapeDtypeStruct((LINE, TOK, DIM), F32),
            jax.ShapeDtypeStruct((LINE, TOK, DIM), BF16),
            jax.ShapeDtypeStruct((LINE - 1, TOK, DIM), BF16),
        ],
        in_specs=[SMEM] * 3 + [VMEM] * 7,
        out_specs=[VMEM] * 4,
        scratch_shapes=[
            pltpu.VMEM((BAND * TOK, DIM), BF16),
            pltpu.VMEM((BAND * TOK, DIM), BF16),
            pltpu.VMEM((DIM, BAND * TOK), BF16),
            pltpu.VMEM((BAND * TOK, DIM), F32),
            pltpu.VMEM((LINE, PAIR, TOK), F32),
            pltpu.VMEM((LINE, PAIR, TOK), F32),
            pltpu.VMEM((LINE, 1, TOK), F32),
            pltpu.VMEM((LINE, 1, TOK), F32),
            pltpu.VMEM((DIM, TOK), F32),
        ],
        compiler_params=pltpu.CompilerParams(vmem_limit_bytes=32 * 1024 * 1024),
        cost_estimate=pl.CostEstimate(flops=10**9, bytes_accessed=6 * 2**20, transcendentals=4 * 10**6),
    )(head, low, weight, start, queries, *keys)


def per_device(seq, dp, teacher_query, teacher_key, student_query, student_key, segment_ids, head_weight):
    to_next, to_second = routes(seq, dp)
    lines = [list(range(i, i + LINE)) for i in range(0, seq, LINE)]
    seq_index = lax.axis_index("seq")
    range_index = seq_index // LINE
    flip = lax.rem(range_index, 2)
    place = lax.rem(seq_index, LINE)
    head = jnp.where(flip == 1, HEADS - 1 - place, place)

    def move(x, route):
        return lax.ppermute(x, AXES, route)

    def exchange(x):
        return lax.all_to_all(x, "seq", 0, 0, axis_index_groups=lines)

    flip, range_index, head = flip.reshape(1), range_index.reshape(1), head.reshape(1)
    own_t, own_s = [exchange(x) for x in pack_keys(flip, teacher_key[0], student_key[0])]
    last_t, last_s = move(own_t, to_next), move(own_s, to_next)
    before = move(jnp.stack([own_t[1:], own_s[1:]]), to_second)
    teacher_query, own_s = lax.optimization_barrier((teacher_query, own_s))
    packed, start, low = pack_queries(flip, range_index, teacher_query[0], student_query[0], segment_ids)
    queries = exchange(packed)
    dq, dk_own, dk_last, dk_before = attend(
        head, low, head_weight, start, queries, own_t, own_s, last_t, last_s, before
    )

    back_last = move(dk_last, reverse(to_next)).astype(F32)
    back_before = move(dk_before, reverse(to_second)).astype(F32)
    dq_home = exchange(dq)
    total = dk_own + back_last + jnp.pad(back_before, ((1, 0), (0, 0), (0, 0)))
    query_grad, key_grad = unpack(flip, dq_home, exchange(total.astype(BF16)))
    return query_grad[None], key_grad[None]


def solution(mesh):
    seq, dp = mesh.shape["seq"], mesh.shape["dp"]
    spec = P("dp", "seq", None)
    return jax.shard_map(
        functools.partial(per_device, seq, dp),
        mesh=mesh,
        in_specs=(spec, spec, spec, spec, P("dp", None), P()),
        out_specs=(spec, spec),
        check_vma=False,
    )
```

```python
import functools
import math

import jax
import jax.numpy as jnp
from jax import lax
from jax.experimental import pallas as pl
from jax.experimental.pallas import tpu as pltpu
from jax.sharding import PartitionSpec as P

HEADS = 4
DIM = 128
TOK = 256
LINE = 4
RING = 8
BEHIND = 7
BAND = 12
OWN = 8
PAIR = 2 * TOK
MASKED = -1e30
F32 = jnp.float32
BF16 = jnp.bfloat16
VMEM = pl.BlockSpec(memory_space=pltpu.VMEM)
SMEM = pl.BlockSpec(memory_space=pltpu.SMEM)
AXES = ("seq", "dp")


def routes(seq, dp):
    last, before_last = [], []
    for ring in range(seq // RING):
        for y in range(RING):
            for part in range(dp):
                me = (ring * RING + y) * dp + part
                ahead = ring + (y >= LINE)
                if ahead < seq // RING:
                    last.append((me, (ahead * RING + RING - 1 - y) * dp + part))
                if ring + 1 < seq // RING:
                    before_last.append((me, ((ring + 1) * RING + y) * dp + part))
    return last, before_last


def reverse(route):
    return [(b, a) for a, b in route]


def head_columns(flip, place):
    head = jnp.where(flip == 1, HEADS - 1 - place, place)
    return pl.ds(pl.multiple_of(head * DIM, DIM), DIM)


def pack_keys_kernel(flip_ref, a_ref, b_ref, out_ref):
    for place in range(HEADS):
        columns = head_columns(flip_ref[0], place)
        out_ref[place, 0] = a_ref[:, columns]
        out_ref[place, 1] = b_ref[:, columns]


def pack_queries_kernel(flip_ref, range_ref, a_ref, b_ref, seg_ref, out_ref, start_ref, low_ref):
    pack_keys_kernel(flip_ref, a_ref, b_ref, out_ref)
    first_block = range_ref[0] * LINE

    def ids(block):
        return seg_ref[0:1, pl.ds(pl.multiple_of(block * TOK, TOK), TOK)]

    own = [ids(first_block + j) for j in range(LINE)]
    ahead = [(first_block - b, ids(jnp.maximum(first_block - b, 0))) for b in range(1, BEHIND + 1)]
    counts = []
    for j in range(LINE):
        first = own[j][:, :1]
        same = jnp.zeros((1, TOK), jnp.int32)
        for i in range(j):
            same += (own[i] == first).astype(jnp.int32)
        for block, row in ahead[: BEHIND - j]:
            same += ((row == first) & (block >= 0)).astype(jnp.int32)
        counts.append(same)
    count = jnp.sum(jnp.concatenate(counts, axis=0), axis=1, keepdims=True)
    seg = jnp.concatenate(own, axis=0)
    column = lax.broadcasted_iota(jnp.int32, (LINE, TOK), 1)
    begin = jnp.where(seg != pltpu.roll(seg, 1, 1), column, 0)
    begin = jnp.where(column == 0, 0, begin)
    step = 1
    while step < TOK:
        begin = jnp.maximum(begin, jnp.where(column >= step, pltpu.roll(begin, step, 1), 0))
        step *= 2
    block_at = (OWN + lax.broadcasted_iota(jnp.int32, (LINE, TOK), 0)) * TOK
    start = block_at + jnp.where(begin > 0, begin, -count)
    start_ref[...] = start
    for j in range(LINE):
        low_ref[j] = jnp.min(start[j : j + 1, :])


def pack_keys(flip, a, b):
    return pl.pallas_call(
        pack_keys_kernel,
        out_shape=jax.ShapeDtypeStruct((HEADS, 2, TOK, DIM), BF16),
        in_specs=[SMEM, VMEM, VMEM],
        out_specs=VMEM,
        cost_estimate=pl.CostEstimate(flops=0, bytes_accessed=2**20, transcendentals=0),
    )(flip, a, b)


def pack_queries(flip, range_index, a, b, seg):
    return pl.pallas_call(
        pack_queries_kernel,
        out_shape=[
            jax.ShapeDtypeStruct((HEADS, 2, TOK, DIM), BF16),
            jax.ShapeDtypeStruct((LINE, TOK), jnp.int32),
            jax.ShapeDtypeStruct((LINE,), jnp.int32),
        ],
        in_specs=[SMEM, SMEM, VMEM, VMEM, VMEM],
        out_specs=[VMEM, VMEM, SMEM],
        cost_estimate=pl.CostEstimate(flops=0, bytes_accessed=2**20, transcendentals=0),
    )(flip, range_index, a, b, seg)


def unpack_kernel(flip_ref, dq_ref, dk_ref, query_ref, key_ref):
    for place in range(HEADS):
        columns = head_columns(flip_ref[0], place)
        query_ref[:, columns] = dq_ref[place].astype(F32)
        key_ref[:, columns] = dk_ref[place].astype(F32)


def unpack(flip, dq, dk):
    return pl.pallas_call(
        unpack_kernel,
        out_shape=[jax.ShapeDtypeStruct((TOK, HEADS * DIM), F32)] * 2,
        in_specs=[SMEM, VMEM, VMEM],
        out_specs=[VMEM] * 2,
        cost_estimate=pl.CostEstimate(flops=0, bytes_accessed=12 * TOK * 512, transcendentals=0),
    )(flip, dq, dk)


def layout_kernel(own_ref, last_ref, before_ref, kt, ks, ks_turned):
    def load(block, teacher, student):
        here = pl.ds(block * TOK, TOK)
        kt[here, :] = teacher
        ks[here, :] = student
        ks_turned[:, here] = student.T

    load(0, jnp.zeros((TOK, DIM), BF16), jnp.zeros((TOK, DIM), BF16))
    for i in range(LINE - 1):
        load(1 + i, before_ref[i, 0], before_ref[i, 1])
    for i in range(LINE):
        load(LINE + i, last_ref[i, 0], last_ref[i, 1])
        load(OWN + i, own_ref[i, 0], own_ref[i, 1])


def layout(own, last, before):
    return pl.pallas_call(
        layout_kernel,
        out_shape=[
            jax.ShapeDtypeStruct((BAND * TOK, DIM), BF16),
            jax.ShapeDtypeStruct((BAND * TOK, DIM), BF16),
            jax.ShapeDtypeStruct((DIM, BAND * TOK), BF16),
        ],
        in_specs=[VMEM] * 3,
        out_specs=[VMEM] * 3,
        compiler_params=pltpu.CompilerParams(vmem_limit_bytes=6 * 1024 * 1024),
        cost_estimate=pl.CostEstimate(flops=10**10, bytes_accessed=16 * 2**20, transcendentals=0),
    )(own, last, before)


def main_kernel(
    head_ref, low_ref, weight_ref, start_ref, query_ref, kt, ks, ks_turned,
    dq_ref, dk_own_ref, dk_last_ref, dk_before_ref,
    dk, et, es, top_t, top_s, dq_acc,
):
    weight = weight_ref[head_ref[0]]
    scale = 1.0 / math.sqrt(DIM)
    pace = scale * math.log2(math.e)
    along_depth = (((1,), (1,)), ((), ()))

    def rows(block):
        return pl.ds(block * TOK, TOK)

    dk[...] = jnp.zeros((BAND * TOK, DIM), F32)
    key_row = lax.broadcasted_iota(jnp.int32, (PAIR, TOK), 0)
    query_column = lax.broadcasted_iota(jnp.int32, (PAIR, TOK), 1)

    for j in range(LINE):
        block = OWN + j
        pairs = (block + 2 - low_ref[j] // TOK) // 2
        q_t, q_s = query_ref[j, 0], query_ref[j, 1]
        start = start_ref[j : j + 1, :]

        def at(t):
            return pl.multiple_of((block - 1 - 2 * t) * TOK, TOK)

        def one(keys, queries, visible, t, top, total, top_out, out):
            s = lax.dot_general(keys, queries, along_depth, preferred_element_type=F32)
            s = jnp.where(visible, s, MASKED)
            new_top = jnp.maximum(top, jnp.max(s, axis=0, keepdims=True))
            e = jnp.exp2((s - new_top) * pace)
            out[t] = e
            top_out[t] = new_top
            return new_top, total * jnp.exp2((top - new_top) * pace) + jnp.sum(e, axis=0, keepdims=True)

        def score(t, visible, carry):
            m_t, l_t, m_s, l_s = carry
            here = pl.ds(at(t), PAIR)
            m_t, l_t = one(kt[here, :], q_t, visible, t, m_t, l_t, top_t, et)
            m_s, l_s = one(ks[here, :], q_s, visible, t, m_s, l_s, top_s, es)
            return m_t, l_t, m_s, l_s

        def score_before(t, carry):
            return score(t, key_row >= start - at(t), carry)

        none, zero = jnp.full((1, TOK), MASKED, F32), jnp.zeros((1, TOK), F32)
        own_visible = (key_row <= query_column + TOK) & (key_row >= start - at(0))
        carry = score(0, own_visible, (none, zero, none, zero))
        m_t, l_t, m_s, l_s = lax.fori_loop(1, pairs, score_before, carry)
        r_t, r_s = weight / l_t, weight / l_s
        dq_acc[...] = jnp.zeros((DIM, TOK), F32)

        def grads(t, _):
            here = pl.ds(at(t), PAIR)
            f_t = jnp.exp2((top_t[t] - m_t) * pace) * r_t
            f_s = jnp.exp2((top_s[t] - m_s) * pace) * r_s
            grad = (es[t] * f_s - et[t] * f_t).astype(BF16)
            dk[here, :] += jnp.dot(grad, q_s, preferred_element_type=F32)
            dq_acc[...] += jnp.dot(ks_turned[:, here], grad, preferred_element_type=F32)
            return 0

        lax.fori_loop(0, pairs, grads, 0)
        dq_ref[j] = (dq_acc[...] * scale).T.astype(BF16)

    for i in range(LINE):
        dk_own_ref[i] = dk[rows(OWN + i), :] * scale
        dk_last_ref[i] = (dk[rows(LINE + i), :] * scale).astype(BF16)
    for i in range(LINE - 1):
        dk_before_ref[i] = (dk[rows(1 + i), :] * scale).astype(BF16)


def attend(head, low, weight, start, queries, *keys):
    return pl.pallas_call(
        main_kernel,
        out_shape=[
            jax.ShapeDtypeStruct((LINE, TOK, DIM), BF16),
            jax.ShapeDtypeStruct((LINE, TOK, DIM), F32),
            jax.ShapeDtypeStruct((LINE, TOK, DIM), BF16),
            jax.ShapeDtypeStruct((LINE - 1, TOK, DIM), BF16),
        ],
        in_specs=[SMEM] * 3 + [VMEM] * 5,
        out_specs=[VMEM] * 4,
        scratch_shapes=[
            pltpu.VMEM((BAND * TOK, DIM), F32),
            pltpu.VMEM((LINE, PAIR, TOK), F32),
            pltpu.VMEM((LINE, PAIR, TOK), F32),
            pltpu.VMEM((LINE, 1, TOK), F32),
            pltpu.VMEM((LINE, 1, TOK), F32),
            pltpu.VMEM((DIM, TOK), F32),
        ],
        compiler_params=pltpu.CompilerParams(vmem_limit_bytes=12 * 1024 * 1024),
        cost_estimate=pl.CostEstimate(flops=10**9, bytes_accessed=6 * 2**20, transcendentals=4 * 10**6),
    )(head, low, weight, start, queries, *keys)


def per_device(seq, dp, teacher_query, teacher_key, student_query, student_key, segment_ids, head_weight):
    to_next, to_second = routes(seq, dp)
    lines = [list(range(i, i + LINE)) for i in range(0, seq, LINE)]
    seq_index = lax.axis_index("seq")
    range_index = seq_index // LINE
    flip = lax.rem(range_index, 2)
    place = lax.rem(seq_index, LINE)
    head = jnp.where(flip == 1, HEADS - 1 - place, place)

    def move(x, route):
        return lax.ppermute(x, AXES, route)

    def exchange(x):
        return lax.all_to_all(x, "seq", 0, 0, axis_index_groups=lines)

    flip, range_index, head = flip.reshape(1), range_index.reshape(1), head.reshape(1)
    own = exchange(pack_keys(flip, teacher_key[0], student_key[0]))
    last = move(own, to_next)
    before = move(own[1:], to_second)
    packed, start, low = pack_queries(flip, range_index, teacher_query[0], student_query[0], segment_ids)
    queries = exchange(packed)
    dq, dk_own, dk_last, dk_before = attend(head, low, head_weight, start, queries, *layout(own, last, before))

    back_last = move(dk_last, reverse(to_next)).astype(F32)
    back_before = move(dk_before, reverse(to_second)).astype(F32)
    dq_home = exchange(dq)
    total = dk_own + back_last + jnp.pad(back_before, ((1, 0), (0, 0), (0, 0)))
    query_grad, key_grad = unpack(flip, dq_home, exchange(total.astype(BF16)))
    return query_grad[None], key_grad[None]


def solution(mesh):
    seq, dp = mesh.shape["seq"], mesh.shape["dp"]
    spec = P("dp", "seq", None)
    return jax.shard_map(
        functools.partial(per_device, seq, dp),
        mesh=mesh,
        in_specs=(spec, spec, spec, spec, P("dp", None), P()),
        out_specs=(spec, spec),
        check_vma=False,
    )
```

```python
import functools
import math

import jax
import jax.numpy as jnp
from jax import lax
from jax.experimental import pallas as pl
from jax.experimental.pallas import tpu as pltpu
from jax.sharding import PartitionSpec as P

HEADS = 4
DIM = 128
TOK = 256
LINE = 4
RING = 8
BEHIND = 7
BAND = 12
OWN = 8
PAIR = 2 * TOK
MASKED = -1e30
F32 = jnp.float32
BF16 = jnp.bfloat16
VMEM = pl.BlockSpec(memory_space=pltpu.VMEM)
SMEM = pl.BlockSpec(memory_space=pltpu.SMEM)
AXES = ("seq", "dp")


def routes(seq, dp):
    rings = seq // RING
    seam = rings // 2 - 1 if dp == 4 else None
    last, before_last, relay = [], [], []
    for ring in range(rings):
        for y in range(RING):
            for part in range(dp):
                me = (ring * RING + y) * dp + part
                ahead = ring + (y >= LINE)
                if ahead < rings:
                    last.append((me, (ahead * RING + RING - 1 - y) * dp + part))
                if ring + 1 < rings:
                    target = ((ring + 1) * RING + y) * dp + part
                    if ring == seam:
                        over = ((rings - 1 if part < 2 else seam) * RING + y) * dp + (part + 2) % 4
                        relay.append((me, over))
                        before_last.append((over, target))
                    else:
                        before_last.append((me, target))
    return last, before_last, relay


def reverse(route):
    return [(b, a) for a, b in route]


def head_columns(flip, place):
    head = jnp.where(flip == 1, HEADS - 1 - place, place)
    return pl.ds(pl.multiple_of(head * DIM, DIM), DIM)


def pack_keys_kernel(flip_ref, a_ref, b_ref, out_ref):
    for place in range(HEADS):
        columns = head_columns(flip_ref[0], place)
        out_ref[place, 0] = a_ref[:, columns]
        out_ref[place, 1] = b_ref[:, columns]


def pack_queries_kernel(flip_ref, range_ref, a_ref, b_ref, seg_ref, out_ref, start_ref, low_ref):
    pack_keys_kernel(flip_ref, a_ref, b_ref, out_ref)
    first_block = range_ref[0] * LINE

    def ids(block):
        return seg_ref[0:1, pl.ds(pl.multiple_of(block * TOK, TOK), TOK)]

    own = [ids(first_block + j) for j in range(LINE)]
    ahead = [(first_block - b, ids(jnp.maximum(first_block - b, 0))) for b in range(1, BEHIND + 1)]
    counts = []
    for j in range(LINE):
        first = own[j][:, :1]
        same = jnp.zeros((1, TOK), jnp.int32)
        for i in range(j):
            same += (own[i] == first).astype(jnp.int32)
        for block, row in ahead[: BEHIND - j]:
            same += ((row == first) & (block >= 0)).astype(jnp.int32)
        counts.append(same)
    count = jnp.sum(jnp.concatenate(counts, axis=0), axis=1, keepdims=True)
    seg = jnp.concatenate(own, axis=0)
    column = lax.broadcasted_iota(jnp.int32, (LINE, TOK), 1)
    begin = jnp.where(seg != pltpu.roll(seg, 1, 1), column, 0)
    begin = jnp.where(column == 0, 0, begin)
    step = 1
    while step < TOK:
        begin = jnp.maximum(begin, jnp.where(column >= step, pltpu.roll(begin, step, 1), 0))
        step *= 2
    block_at = (OWN + lax.broadcasted_iota(jnp.int32, (LINE, TOK), 0)) * TOK
    start = block_at + jnp.where(begin > 0, begin, -count)
    start_ref[...] = start
    for j in range(LINE):
        low_ref[j] = jnp.min(start[j : j + 1, :])


def pack_keys(flip, a, b):
    return pl.pallas_call(
        pack_keys_kernel,
        out_shape=jax.ShapeDtypeStruct((HEADS, 2, TOK, DIM), BF16),
        in_specs=[SMEM, VMEM, VMEM],
        out_specs=VMEM,
        cost_estimate=pl.CostEstimate(flops=0, bytes_accessed=2**20, transcendentals=0),
    )(flip, a, b)


def pack_queries(flip, range_index, a, b, seg):
    return pl.pallas_call(
        pack_queries_kernel,
        out_shape=[
            jax.ShapeDtypeStruct((HEADS, 2, TOK, DIM), BF16),
            jax.ShapeDtypeStruct((LINE, TOK), jnp.int32),
            jax.ShapeDtypeStruct((LINE,), jnp.int32),
        ],
        in_specs=[SMEM, SMEM, VMEM, VMEM, VMEM],
        out_specs=[VMEM, VMEM, SMEM],
        cost_estimate=pl.CostEstimate(flops=0, bytes_accessed=2**20, transcendentals=0),
    )(flip, range_index, a, b, seg)


def unpack_kernel(flip_ref, dq_ref, dk_ref, query_ref, key_ref):
    for place in range(HEADS):
        columns = head_columns(flip_ref[0], place)
        query_ref[:, columns] = dq_ref[place].astype(F32)
        key_ref[:, columns] = dk_ref[place].astype(F32)


def unpack(flip, dq, dk):
    return pl.pallas_call(
        unpack_kernel,
        out_shape=[jax.ShapeDtypeStruct((TOK, HEADS * DIM), F32)] * 2,
        in_specs=[SMEM, VMEM, VMEM],
        out_specs=[VMEM] * 2,
        cost_estimate=pl.CostEstimate(flops=0, bytes_accessed=12 * TOK * 512, transcendentals=0),
    )(flip, dq, dk)


def layout_kernel(own_ref, last_ref, before_ref, kt, ks):
    def load(block, teacher, student):
        here = pl.ds(block * TOK, TOK)
        kt[here, :] = teacher
        ks[here, :] = student

    load(0, jnp.zeros((TOK, DIM), BF16), jnp.zeros((TOK, DIM), BF16))
    for i in range(LINE - 1):
        load(1 + i, before_ref[i, 0], before_ref[i, 1])
    for i in range(LINE):
        load(LINE + i, last_ref[i, 0], last_ref[i, 1])
        load(OWN + i, own_ref[i, 0], own_ref[i, 1])


def layout(own, last, before):
    return pl.pallas_call(
        layout_kernel,
        out_shape=[
            jax.ShapeDtypeStruct((BAND * TOK, DIM), BF16),
            jax.ShapeDtypeStruct((BAND * TOK, DIM), BF16),
        ],
        in_specs=[VMEM] * 3,
        out_specs=[VMEM] * 2,
        compiler_params=pltpu.CompilerParams(vmem_limit_bytes=6 * 1024 * 1024),
        cost_estimate=pl.CostEstimate(flops=10**10, bytes_accessed=16 * 2**20, transcendentals=0),
    )(own, last, before)


def main_kernel(
    head_ref, low_ref, weight_ref, start_ref, query_ref, kt, ks,
    dq_ref, dk_own_ref, dk_last_ref, dk_before_ref,
    ks_turned, dk, et, es, top_t, top_s, dq_acc,
):
    weight = weight_ref[head_ref[0]]
    scale = 1.0 / math.sqrt(DIM)
    pace = scale * math.log2(math.e)
    along_depth = (((1,), (1,)), ((), ()))

    def rows(block):
        return pl.ds(block * TOK, TOK)

    dk[...] = jnp.zeros((BAND * TOK, DIM), F32)
    for block in range(BAND):
        ks_turned[:, rows(block)] = ks[rows(block), :].T
    key_row = lax.broadcasted_iota(jnp.int32, (PAIR, TOK), 0)
    query_column = lax.broadcasted_iota(jnp.int32, (PAIR, TOK), 1)

    for j in range(LINE):
        block = OWN + j
        pairs = (block + 2 - low_ref[j] // TOK) // 2
        q_t, q_s = query_ref[j, 0], query_ref[j, 1]
        start = start_ref[j : j + 1, :]

        def at(t):
            return pl.multiple_of((block - 1 - 2 * t) * TOK, TOK)

        def one(keys, queries, visible, t, top, total, top_out, out):
            s = lax.dot_general(keys, queries, along_depth, preferred_element_type=F32)
            s = jnp.where(visible, s, MASKED)
            new_top = jnp.maximum(top, jnp.max(s, axis=0, keepdims=True))
            e = jnp.exp2((s - new_top) * pace)
            out[t] = e
            top_out[t] = new_top
            return new_top, total * jnp.exp2((top - new_top) * pace) + jnp.sum(e, axis=0, keepdims=True)

        def score(t, visible, carry):
            m_t, l_t, m_s, l_s = carry
            here = pl.ds(at(t), PAIR)
            m_t, l_t = one(kt[here, :], q_t, visible, t, m_t, l_t, top_t, et)
            m_s, l_s = one(ks[here, :], q_s, visible, t, m_s, l_s, top_s, es)
            return m_t, l_t, m_s, l_s

        def score_before(t, carry):
            return score(t, key_row >= start - at(t), carry)

        none, zero = jnp.full((1, TOK), MASKED, F32), jnp.zeros((1, TOK), F32)
        own_visible = (key_row <= query_column + TOK) & (key_row >= start - at(0))
        carry = score(0, own_visible, (none, zero, none, zero))
        m_t, l_t, m_s, l_s = lax.fori_loop(1, pairs, score_before, carry)
        r_t, r_s = weight / l_t, weight / l_s
        dq_acc[...] = jnp.zeros((DIM, TOK), F32)

        def grads(t, _):
            here = pl.ds(at(t), PAIR)
            f_t = jnp.exp2((top_t[t] - m_t) * pace) * r_t
            f_s = jnp.exp2((top_s[t] - m_s) * pace) * r_s
            grad = (es[t] * f_s - et[t] * f_t).astype(BF16)
            dk[here, :] += jnp.dot(grad, q_s, preferred_element_type=F32)
            dq_acc[...] += jnp.dot(ks_turned[:, here], grad, preferred_element_type=F32)
            return 0

        lax.fori_loop(0, pairs, grads, 0)
        dq_ref[j] = (dq_acc[...] * scale).T.astype(BF16)

    for i in range(LINE):
        dk_own_ref[i] = dk[rows(OWN + i), :] * scale
        dk_last_ref[i] = (dk[rows(LINE + i), :] * scale).astype(BF16)
    for i in range(LINE - 1):
        dk_before_ref[i] = (dk[rows(1 + i), :] * scale).astype(BF16)


def attend(head, low, weight, start, queries, *keys):
    return pl.pallas_call(
        main_kernel,
        out_shape=[
            jax.ShapeDtypeStruct((LINE, TOK, DIM), BF16),
            jax.ShapeDtypeStruct((LINE, TOK, DIM), F32),
            jax.ShapeDtypeStruct((LINE, TOK, DIM), BF16),
            jax.ShapeDtypeStruct((LINE - 1, TOK, DIM), BF16),
        ],
        in_specs=[SMEM] * 3 + [VMEM] * 4,
        out_specs=[VMEM] * 4,
        scratch_shapes=[
            pltpu.VMEM((DIM, BAND * TOK), BF16),
            pltpu.VMEM((BAND * TOK, DIM), F32),
            pltpu.VMEM((LINE, PAIR, TOK), F32),
            pltpu.VMEM((LINE, PAIR, TOK), F32),
            pltpu.VMEM((LINE, 1, TOK), F32),
            pltpu.VMEM((LINE, 1, TOK), F32),
            pltpu.VMEM((DIM, TOK), F32),
        ],
        compiler_params=pltpu.CompilerParams(vmem_limit_bytes=12 * 1024 * 1024),
        cost_estimate=pl.CostEstimate(flops=10**9, bytes_accessed=6 * 2**20, transcendentals=4 * 10**6),
    )(head, low, weight, start, queries, *keys)


def per_device(seq, dp, teacher_query, teacher_key, student_query, student_key, segment_ids, head_weight):
    to_next, to_second, relay = routes(seq, dp)
    to_second_straight = [(i, i + RING * dp) for i in range((seq - RING) * dp)]
    lines = [list(range(i, i + LINE)) for i in range(0, seq, LINE)]
    seq_index = lax.axis_index("seq")
    range_index = seq_index // LINE
    flip = lax.rem(range_index, 2)
    place = lax.rem(seq_index, LINE)
    head = jnp.where(flip == 1, HEADS - 1 - place, place)

    def move(x, route):
        return lax.ppermute(x, AXES, route)

    def exchange(x):
        return lax.all_to_all(x, "seq", 0, 0, axis_index_groups=lines)

    flip, range_index, head = flip.reshape(1), range_index.reshape(1), head.reshape(1)
    own = exchange(pack_keys(flip, teacher_key[0], student_key[0]))
    last = move(own, to_next)
    parting = own[1:]
    if relay:
        ring, pair = seq_index // RING, lax.axis_index("dp") // 2
        relays = ((ring == seq // RING - 1) & (pair == 1)) | ((ring == seq // RING // 2 - 1) & (pair == 0))
        parting = jnp.where(relays, move(parting, relay), parting)
    before = move(parting, to_second)
    packed, start, low = pack_queries(flip, range_index, teacher_query[0], student_query[0], segment_ids)
    queries = exchange(packed)
    dq, dk_own, dk_last, dk_before = attend(head, low, head_weight, start, queries, *layout(own, last, before))

    back_last = move(dk_last, reverse(to_next)).astype(F32)
    back_before = move(dk_before, reverse(to_second_straight)).astype(F32)
    dq_home = exchange(dq)
    total = dk_own + back_last + jnp.pad(back_before, ((1, 0), (0, 0), (0, 0)))
    query_grad, key_grad = unpack(flip, dq_home, exchange(total.astype(BF16)))
    return query_grad[None], key_grad[None]


def solution(mesh):
    seq, dp = mesh.shape["seq"], mesh.shape["dp"]
    spec = P("dp", "seq", None)
    return jax.shard_map(
        functools.partial(per_device, seq, dp),
        mesh=mesh,
        in_specs=(spec, spec, spec, spec, P("dp", None), P()),
        out_specs=(spec, spec),
        check_vma=False,
    )
```

```python
import functools
import math

import jax
import jax.numpy as jnp
from jax import lax
from jax.experimental import pallas as pl
from jax.experimental.pallas import tpu as pltpu
from jax.sharding import PartitionSpec as P

HEADS = 4
DIM = 128
TOK = 256
LINE = 4
RING = 8
BEHIND = 7
BAND = 12
OWN = 8
PAIR = 2 * TOK
MASKED = -1e30
F32 = jnp.float32
BF16 = jnp.bfloat16
VMEM = pl.BlockSpec(memory_space=pltpu.VMEM)
SMEM = pl.BlockSpec(memory_space=pltpu.SMEM)
AXES = ("seq", "dp")


def routes(seq, dp):
    rings = seq // RING
    seam = rings // 2 - 1 if dp == 4 else None
    last, before_last, relay = [], [], []
    for ring in range(rings):
        for y in range(RING):
            for part in range(dp):
                me = (ring * RING + y) * dp + part
                ahead = ring + (y >= LINE)
                if ahead < rings:
                    last.append((me, (ahead * RING + RING - 1 - y) * dp + part))
                if ring + 1 < rings:
                    target = ((ring + 1) * RING + y) * dp + part
                    if ring == seam:
                        over = ((rings - 1) * RING + y) * dp + part
                        relay.append((me, over))
                        before_last.append((over, target))
                    else:
                        before_last.append((me, target))
    return last, before_last, relay


def reverse(route):
    return [(b, a) for a, b in route]


def head_columns(flip, place):
    head = jnp.where(flip == 1, HEADS - 1 - place, place)
    return pl.ds(pl.multiple_of(head * DIM, DIM), DIM)


def pack_kernel(flip_ref, a_ref, b_ref, c_ref, d_ref, keys_ref, queries_ref):
    for place in range(HEADS):
        columns = head_columns(flip_ref[0], place)
        keys_ref[place, 0] = a_ref[:, columns]
        keys_ref[place, 1] = b_ref[:, columns]
        queries_ref[place, 0] = c_ref[:, columns]
        queries_ref[place, 1] = d_ref[:, columns]


def pack(flip, *states):
    return pl.pallas_call(
        pack_kernel,
        out_shape=[jax.ShapeDtypeStruct((HEADS, 2, TOK, DIM), BF16)] * 2,
        in_specs=[SMEM] + [VMEM] * 4,
        out_specs=[VMEM] * 2,
        cost_estimate=pl.CostEstimate(flops=0, bytes_accessed=2**21, transcendentals=0),
    )(flip, *states)


def starts_kernel(range_ref, seg_ref, start_ref, low_ref):
    first_block = range_ref[0] * LINE

    def ids(block):
        return seg_ref[0:1, pl.ds(pl.multiple_of(block * TOK, TOK), TOK)]

    own = [ids(first_block + j) for j in range(LINE)]
    ahead = [(first_block - b, ids(jnp.maximum(first_block - b, 0))) for b in range(1, BEHIND + 1)]
    counts = []
    for j in range(LINE):
        first = own[j][:, :1]
        same = jnp.zeros((1, TOK), jnp.int32)
        for i in range(j):
            same += (own[i] == first).astype(jnp.int32)
        for block, row in ahead[: BEHIND - j]:
            same += ((row == first) & (block >= 0)).astype(jnp.int32)
        counts.append(same)
    count = jnp.sum(jnp.concatenate(counts, axis=0), axis=1, keepdims=True)
    seg = jnp.concatenate(own, axis=0)
    column = lax.broadcasted_iota(jnp.int32, (LINE, TOK), 1)
    begin = jnp.where(seg != pltpu.roll(seg, 1, 1), column, 0)
    begin = jnp.where(column == 0, 0, begin)
    step = 1
    while step < TOK:
        begin = jnp.maximum(begin, jnp.where(column >= step, pltpu.roll(begin, step, 1), 0))
        step *= 2
    block_at = (OWN + lax.broadcasted_iota(jnp.int32, (LINE, TOK), 0)) * TOK
    start = block_at + jnp.where(begin > 0, begin, -count)
    start_ref[...] = start
    for j in range(LINE):
        low_ref[j] = jnp.min(start[j : j + 1, :])


def starts(range_index, seg):
    return pl.pallas_call(
        starts_kernel,
        out_shape=[jax.ShapeDtypeStruct((LINE, TOK), jnp.int32), jax.ShapeDtypeStruct((LINE,), jnp.int32)],
        in_specs=[SMEM, VMEM],
        out_specs=[VMEM, SMEM],
        cost_estimate=pl.CostEstimate(flops=0, bytes_accessed=2**20, transcendentals=0),
    )(range_index, seg)


def unpack_kernel(flip_ref, dq_ref, dk_ref, query_ref, key_ref):
    for place in range(HEADS):
        columns = head_columns(flip_ref[0], place)
        query_ref[:, columns] = dq_ref[place].astype(F32)
        key_ref[:, columns] = dk_ref[place].astype(F32)


def unpack(flip, dq, dk):
    return pl.pallas_call(
        unpack_kernel,
        out_shape=[jax.ShapeDtypeStruct((TOK, HEADS * DIM), F32)] * 2,
        in_specs=[SMEM, VMEM, VMEM],
        out_specs=[VMEM] * 2,
        cost_estimate=pl.CostEstimate(flops=0, bytes_accessed=12 * TOK * 512, transcendentals=0),
    )(flip, dq, dk)


def layout_kernel(own_ref, last_ref, before_ref, kt, ks):
    def load(block, teacher, student):
        here = pl.ds(block * TOK, TOK)
        kt[here, :] = teacher
        ks[here, :] = student

    load(0, jnp.zeros((TOK, DIM), BF16), jnp.zeros((TOK, DIM), BF16))
    for i in range(LINE - 1):
        load(1 + i, before_ref[i, 0], before_ref[i, 1])
    for i in range(LINE):
        load(LINE + i, last_ref[i, 0], last_ref[i, 1])
        load(OWN + i, own_ref[i, 0], own_ref[i, 1])


def layout(own, last, before):
    return pl.pallas_call(
        layout_kernel,
        out_shape=[
            jax.ShapeDtypeStruct((BAND * TOK, DIM), BF16),
            jax.ShapeDtypeStruct((BAND * TOK, DIM), BF16),
        ],
        in_specs=[VMEM] * 3,
        out_specs=[VMEM] * 2,
        compiler_params=pltpu.CompilerParams(vmem_limit_bytes=6 * 1024 * 1024),
        cost_estimate=pl.CostEstimate(flops=10**10, bytes_accessed=16 * 2**20, transcendentals=0),
    )(own, last, before)


def main_kernel(
    head_ref, low_ref, weight_ref, start_ref, query_ref, kt, ks,
    dq_ref, dk_own_ref, dk_last_ref, dk_before_ref,
    ks_turned, dk, et, es, top_t, top_s, dq_acc,
):
    weight = weight_ref[head_ref[0]]
    scale = 1.0 / math.sqrt(DIM)
    pace = scale * math.log2(math.e)
    along_depth = (((1,), (1,)), ((), ()))

    def rows(block):
        return pl.ds(block * TOK, TOK)

    dk[...] = jnp.zeros((BAND * TOK, DIM), F32)
    for block in range(BAND):
        ks_turned[:, rows(block)] = ks[rows(block), :].T
    key_row = lax.broadcasted_iota(jnp.int32, (PAIR, TOK), 0)
    query_column = lax.broadcasted_iota(jnp.int32, (PAIR, TOK), 1)

    for j in range(LINE):
        block = OWN + j
        pairs = (block + 2 - low_ref[j] // TOK) // 2
        q_t, q_s = query_ref[j, 0], query_ref[j, 1]
        start = start_ref[j : j + 1, :]

        def at(t):
            return pl.multiple_of((block - 1 - 2 * t) * TOK, TOK)

        def one(keys, queries, visible, t, top, total, top_out, out):
            s = lax.dot_general(keys, queries, along_depth, preferred_element_type=F32)
            s = jnp.where(visible, s, MASKED)
            new_top = jnp.maximum(top, jnp.max(s, axis=0, keepdims=True))
            e = jnp.exp2((s - new_top) * pace)
            out[t] = e
            top_out[t] = new_top
            return new_top, total * jnp.exp2((top - new_top) * pace) + jnp.sum(e, axis=0, keepdims=True)

        def score(t, visible, carry):
            m_t, l_t, m_s, l_s = carry
            here = pl.ds(at(t), PAIR)
            m_t, l_t = one(kt[here, :], q_t, visible, t, m_t, l_t, top_t, et)
            m_s, l_s = one(ks[here, :], q_s, visible, t, m_s, l_s, top_s, es)
            return m_t, l_t, m_s, l_s

        def score_before(t, carry):
            return score(t, key_row >= start - at(t), carry)

        none, zero = jnp.full((1, TOK), MASKED, F32), jnp.zeros((1, TOK), F32)
        own_visible = (key_row <= query_column + TOK) & (key_row >= start - at(0))
        carry = score(0, own_visible, (none, zero, none, zero))
        m_t, l_t, m_s, l_s = lax.fori_loop(1, pairs, score_before, carry)
        r_t, r_s = weight / l_t, weight / l_s
        dq_acc[...] = jnp.zeros((DIM, TOK), F32)

        def grads(t, _):
            here = pl.ds(at(t), PAIR)
            f_t = jnp.exp2((top_t[t] - m_t) * pace) * r_t
            f_s = jnp.exp2((top_s[t] - m_s) * pace) * r_s
            grad = (es[t] * f_s - et[t] * f_t).astype(BF16)
            dk[here, :] += jnp.dot(grad, q_s, preferred_element_type=F32)
            dq_acc[...] += jnp.dot(ks_turned[:, here], grad, preferred_element_type=F32)
            return 0

        lax.fori_loop(0, pairs, grads, 0)
        dq_ref[j] = (dq_acc[...] * scale).T.astype(BF16)

    for i in range(LINE):
        dk_own_ref[i] = dk[rows(OWN + i), :] * scale
        dk_last_ref[i] = (dk[rows(LINE + i), :] * scale).astype(BF16)
    for i in range(LINE - 1):
        dk_before_ref[i] = (dk[rows(1 + i), :] * scale).astype(BF16)


def attend(head, low, weight, start, queries, *keys):
    return pl.pallas_call(
        main_kernel,
        out_shape=[
            jax.ShapeDtypeStruct((LINE, TOK, DIM), BF16),
            jax.ShapeDtypeStruct((LINE, TOK, DIM), F32),
            jax.ShapeDtypeStruct((LINE, TOK, DIM), BF16),
            jax.ShapeDtypeStruct((LINE - 1, TOK, DIM), BF16),
        ],
        in_specs=[SMEM] * 3 + [VMEM] * 4,
        out_specs=[VMEM] * 4,
        scratch_shapes=[
            pltpu.VMEM((DIM, BAND * TOK), BF16),
            pltpu.VMEM((BAND * TOK, DIM), F32),
            pltpu.VMEM((LINE, PAIR, TOK), F32),
            pltpu.VMEM((LINE, PAIR, TOK), F32),
            pltpu.VMEM((LINE, 1, TOK), F32),
            pltpu.VMEM((LINE, 1, TOK), F32),
            pltpu.VMEM((DIM, TOK), F32),
        ],
        compiler_params=pltpu.CompilerParams(vmem_limit_bytes=12 * 1024 * 1024),
        cost_estimate=pl.CostEstimate(flops=10**9, bytes_accessed=6 * 2**20, transcendentals=4 * 10**6),
    )(head, low, weight, start, queries, *keys)


def per_device(seq, dp, teacher_query, teacher_key, student_query, student_key, segment_ids, head_weight):
    to_next, to_second, relay = routes(seq, dp)
    to_second_straight = [(i, i + RING * dp) for i in range((seq - RING) * dp)]
    lines = [list(range(i, i + LINE)) for i in range(0, seq, LINE)]
    seq_index = lax.axis_index("seq")
    range_index = seq_index // LINE
    flip = lax.rem(range_index, 2)
    place = lax.rem(seq_index, LINE)
    head = jnp.where(flip == 1, HEADS - 1 - place, place)

    def move(x, route):
        return lax.ppermute(x, AXES, route)

    def exchange(x):
        return lax.all_to_all(x, "seq", 0, 0, axis_index_groups=lines)

    flip, range_index, head = flip.reshape(1), range_index.reshape(1), head.reshape(1)
    keys, queries = pack(flip, teacher_key[0], student_key[0], teacher_query[0], student_query[0])
    own = exchange(keys)
    last = move(own, to_next)
    parting = own[1:]
    if relay:
        relays = seq_index >= seq - RING
        parting = jnp.where(relays, move(parting, relay), parting)
    before = move(parting, to_second)
    start, low = starts(range_index, segment_ids)
    queries = exchange(queries)
    dq, dk_own, dk_last, dk_before = attend(head, low, head_weight, start, queries, *layout(own, last, before))

    back_last = move(dk_last, reverse(to_next)).astype(F32)
    back_before = move(dk_before, reverse(to_second_straight)).astype(F32)
    dq_home = exchange(dq)
    total = dk_own + back_last + jnp.pad(back_before, ((1, 0), (0, 0), (0, 0)))
    query_grad, key_grad = unpack(flip, dq_home, exchange(total.astype(BF16)))
    return query_grad[None], key_grad[None]


def solution(mesh):
    seq, dp = mesh.shape["seq"], mesh.shape["dp"]
    spec = P("dp", "seq", None)
    return jax.shard_map(
        functools.partial(per_device, seq, dp),
        mesh=mesh,
        in_specs=(spec, spec, spec, spec, P("dp", None), P()),
        out_specs=(spec, spec),
        check_vma=False,
    )
```

```python
import functools
import math

import jax
import jax.numpy as jnp
from jax import lax
from jax.experimental import pallas as pl
from jax.experimental.pallas import tpu as pltpu
from jax.sharding import PartitionSpec as P

HEADS = 4
DIM = 128
TOK = 256
LINE = 4
RING = 8
BEHIND = 7
BAND = 12
OWN = 8
PAIR = 2 * TOK
MASKED = -1e30
F32 = jnp.float32
BF16 = jnp.bfloat16
VMEM = pl.BlockSpec(memory_space=pltpu.VMEM)
SMEM = pl.BlockSpec(memory_space=pltpu.SMEM)
AXES = ("seq", "dp")


def routes(seq, dp):
    rings = seq // RING
    seam = rings // 2 - 1 if dp == 4 else None
    last, before_last, relay, cross = [], [], [], []
    for ring in range(rings):
        for y in range(RING):
            for part in range(dp):
                me = (ring * RING + y) * dp + part
                ahead = ring + (y >= LINE)
                if ahead < rings:
                    last.append((me, (ahead * RING + RING - 1 - y) * dp + part))
                if ring + 1 < rings:
                    target = ((ring + 1) * RING + y) * dp + part
                    if ring == seam:
                        relay.append((me, y * dp + part))
                        cross.append((y * dp + part, target))
                    else:
                        before_last.append((me, target))
    return last, before_last, relay, cross


def reverse(route):
    return [(b, a) for a, b in route]


def head_columns(flip, place):
    head = jnp.where(flip == 1, HEADS - 1 - place, place)
    return pl.ds(pl.multiple_of(head * DIM, DIM), DIM)


def pack_kernel(flip_ref, a_ref, b_ref, c_ref, d_ref, keys_ref, queries_ref):
    for place in range(HEADS):
        columns = head_columns(flip_ref[0], place)
        keys_ref[place, 0] = a_ref[:, columns]
        keys_ref[place, 1] = b_ref[:, columns]
        queries_ref[place, 0] = c_ref[:, columns]
        queries_ref[place, 1] = d_ref[:, columns]


def pack(flip, *states):
    return pl.pallas_call(
        pack_kernel,
        out_shape=[jax.ShapeDtypeStruct((HEADS, 2, TOK, DIM), BF16)] * 2,
        in_specs=[SMEM] + [VMEM] * 4,
        out_specs=[VMEM] * 2,
        cost_estimate=pl.CostEstimate(flops=0, bytes_accessed=2**21, transcendentals=0),
    )(flip, *states)


def starts_kernel(range_ref, seg_ref, start_ref, low_ref):
    first_block = range_ref[0] * LINE

    def ids(block):
        return seg_ref[0:1, pl.ds(pl.multiple_of(block * TOK, TOK), TOK)]

    own = [ids(first_block + j) for j in range(LINE)]
    ahead = [(first_block - b, ids(jnp.maximum(first_block - b, 0))) for b in range(1, BEHIND + 1)]
    counts = []
    for j in range(LINE):
        first = own[j][:, :1]
        same = jnp.zeros((1, TOK), jnp.int32)
        for i in range(j):
            same += (own[i] == first).astype(jnp.int32)
        for block, row in ahead[: BEHIND - j]:
            same += ((row == first) & (block >= 0)).astype(jnp.int32)
        counts.append(same)
    count = jnp.sum(jnp.concatenate(counts, axis=0), axis=1, keepdims=True)
    seg = jnp.concatenate(own, axis=0)
    column = lax.broadcasted_iota(jnp.int32, (LINE, TOK), 1)
    begin = jnp.where(seg != pltpu.roll(seg, 1, 1), column, 0)
    begin = jnp.where(column == 0, 0, begin)
    step = 1
    while step < TOK:
        begin = jnp.maximum(begin, jnp.where(column >= step, pltpu.roll(begin, step, 1), 0))
        step *= 2
    block_at = (OWN + lax.broadcasted_iota(jnp.int32, (LINE, TOK), 0)) * TOK
    start = block_at + jnp.where(begin > 0, begin, -count)
    start_ref[...] = start
    for j in range(LINE):
        low_ref[j] = jnp.min(start[j : j + 1, :])


def starts(range_index, seg):
    return pl.pallas_call(
        starts_kernel,
        out_shape=[jax.ShapeDtypeStruct((LINE, TOK), jnp.int32), jax.ShapeDtypeStruct((LINE,), jnp.int32)],
        in_specs=[SMEM, VMEM],
        out_specs=[VMEM, SMEM],
        cost_estimate=pl.CostEstimate(flops=0, bytes_accessed=2**20, transcendentals=0),
    )(range_index, seg)


def unpack_kernel(flip_ref, dq_ref, dk_ref, query_ref, key_ref):
    for place in range(HEADS):
        columns = head_columns(flip_ref[0], place)
        query_ref[:, columns] = dq_ref[place].astype(F32)
        key_ref[:, columns] = dk_ref[place].astype(F32)


def unpack(flip, dq, dk):
    return pl.pallas_call(
        unpack_kernel,
        out_shape=[jax.ShapeDtypeStruct((TOK, HEADS * DIM), F32)] * 2,
        in_specs=[SMEM, VMEM, VMEM],
        out_specs=[VMEM] * 2,
        cost_estimate=pl.CostEstimate(flops=0, bytes_accessed=12 * TOK * 512, transcendentals=0),
    )(flip, dq, dk)


def layout_kernel(crossed_ref, own_ref, last_ref, before_ref, cross_ref, kt, ks):
    def load(block, teacher, student):
        here = pl.ds(block * TOK, TOK)
        kt[here, :] = teacher
        ks[here, :] = student

    load(0, jnp.zeros((TOK, DIM), BF16), jnp.zeros((TOK, DIM), BF16))
    crossed = crossed_ref[0] == 1

    @pl.when(crossed)
    def _():
        for i in range(LINE - 1):
            load(1 + i, cross_ref[i, 0], cross_ref[i, 1])

    @pl.when(jnp.logical_not(crossed))
    def _():
        for i in range(LINE - 1):
            load(1 + i, before_ref[i, 0], before_ref[i, 1])

    for i in range(LINE):
        load(LINE + i, last_ref[i, 0], last_ref[i, 1])
        load(OWN + i, own_ref[i, 0], own_ref[i, 1])


def layout(crossed, own, last, before, cross):
    return pl.pallas_call(
        layout_kernel,
        out_shape=[
            jax.ShapeDtypeStruct((BAND * TOK, DIM), BF16),
            jax.ShapeDtypeStruct((BAND * TOK, DIM), BF16),
        ],
        in_specs=[SMEM] + [VMEM] * 4,
        out_specs=[VMEM] * 2,
        compiler_params=pltpu.CompilerParams(vmem_limit_bytes=6 * 1024 * 1024),
        cost_estimate=pl.CostEstimate(flops=10**10, bytes_accessed=16 * 2**20, transcendentals=0),
    )(crossed, own, last, before, cross)


def main_kernel(
    head_ref, low_ref, weight_ref, start_ref, query_ref, kt, ks,
    dq_ref, dk_own_ref, dk_last_ref, dk_before_ref,
    ks_turned, dk, et, es, top_t, top_s, dq_acc,
):
    weight = weight_ref[head_ref[0]]
    scale = 1.0 / math.sqrt(DIM)
    pace = scale * math.log2(math.e)
    along_depth = (((1,), (1,)), ((), ()))

    def rows(block):
        return pl.ds(block * TOK, TOK)

    dk[...] = jnp.zeros((BAND * TOK, DIM), F32)
    for block in range(BAND):
        ks_turned[:, rows(block)] = ks[rows(block), :].T
    key_row = lax.broadcasted_iota(jnp.int32, (PAIR, TOK), 0)
    query_column = lax.broadcasted_iota(jnp.int32, (PAIR, TOK), 1)

    for j in range(LINE):
        block = OWN + j
        pairs = (block + 2 - low_ref[j] // TOK) // 2
        q_t, q_s = query_ref[j, 0], query_ref[j, 1]
        start = start_ref[j : j + 1, :]

        def at(t):
            return pl.multiple_of((block - 1 - 2 * t) * TOK, TOK)

        def one(keys, queries, visible, t, top, total, top_out, out):
            s = lax.dot_general(keys, queries, along_depth, preferred_element_type=F32)
            s = jnp.where(visible, s, MASKED)
            new_top = jnp.maximum(top, jnp.max(s, axis=0, keepdims=True))
            e = jnp.exp2((s - new_top) * pace)
            out[t] = e
            top_out[t] = new_top
            return new_top, total * jnp.exp2((top - new_top) * pace) + jnp.sum(e, axis=0, keepdims=True)

        def score(t, visible, carry):
            m_t, l_t, m_s, l_s = carry
            here = pl.ds(at(t), PAIR)
            m_t, l_t = one(kt[here, :], q_t, visible, t, m_t, l_t, top_t, et)
            m_s, l_s = one(ks[here, :], q_s, visible, t, m_s, l_s, top_s, es)
            return m_t, l_t, m_s, l_s

        def score_before(t, carry):
            return score(t, key_row >= start - at(t), carry)

        none, zero = jnp.full((1, TOK), MASKED, F32), jnp.zeros((1, TOK), F32)
        own_visible = (key_row <= query_column + TOK) & (key_row >= start - at(0))
        carry = score(0, own_visible, (none, zero, none, zero))
        m_t, l_t, m_s, l_s = lax.fori_loop(1, pairs, score_before, carry)
        r_t, r_s = weight / l_t, weight / l_s
        dq_acc[...] = jnp.zeros((DIM, TOK), F32)

        def grads(t, _):
            here = pl.ds(at(t), PAIR)
            f_t = jnp.exp2((top_t[t] - m_t) * pace) * r_t
            f_s = jnp.exp2((top_s[t] - m_s) * pace) * r_s
            grad = (es[t] * f_s - et[t] * f_t).astype(BF16)
            dk[here, :] += jnp.dot(grad, q_s, preferred_element_type=F32)
            dq_acc[...] += jnp.dot(ks_turned[:, here], grad, preferred_element_type=F32)
            return 0

        lax.fori_loop(0, pairs, grads, 0)
        dq_ref[j] = (dq_acc[...] * scale).T.astype(BF16)

    for i in range(LINE):
        dk_own_ref[i] = dk[rows(OWN + i), :] * scale
        dk_last_ref[i] = (dk[rows(LINE + i), :] * scale).astype(BF16)
    for i in range(LINE - 1):
        dk_before_ref[i] = (dk[rows(1 + i), :] * scale).astype(BF16)


def attend(head, low, weight, start, queries, *keys):
    return pl.pallas_call(
        main_kernel,
        out_shape=[
            jax.ShapeDtypeStruct((LINE, TOK, DIM), BF16),
            jax.ShapeDtypeStruct((LINE, TOK, DIM), F32),
            jax.ShapeDtypeStruct((LINE, TOK, DIM), BF16),
            jax.ShapeDtypeStruct((LINE - 1, TOK, DIM), BF16),
        ],
        in_specs=[SMEM] * 3 + [VMEM] * 4,
        out_specs=[VMEM] * 4,
        scratch_shapes=[
            pltpu.VMEM((DIM, BAND * TOK), BF16),
            pltpu.VMEM((BAND * TOK, DIM), F32),
            pltpu.VMEM((LINE, PAIR, TOK), F32),
            pltpu.VMEM((LINE, PAIR, TOK), F32),
            pltpu.VMEM((LINE, 1, TOK), F32),
            pltpu.VMEM((LINE, 1, TOK), F32),
            pltpu.VMEM((DIM, TOK), F32),
        ],
        compiler_params=pltpu.CompilerParams(vmem_limit_bytes=12 * 1024 * 1024),
        cost_estimate=pl.CostEstimate(flops=10**9, bytes_accessed=6 * 2**20, transcendentals=4 * 10**6),
    )(head, low, weight, start, queries, *keys)


def per_device(seq, dp, teacher_query, teacher_key, student_query, student_key, segment_ids, head_weight):
    to_next, to_second, relay, to_cross = routes(seq, dp)
    to_second_straight = [(i, i + RING * dp) for i in range((seq - RING) * dp)]
    lines = [list(range(i, i + LINE)) for i in range(0, seq, LINE)]
    seq_index = lax.axis_index("seq")
    range_index = seq_index // LINE
    flip = lax.rem(range_index, 2)
    place = lax.rem(seq_index, LINE)
    head = jnp.where(flip == 1, HEADS - 1 - place, place)

    def move(x, route):
        return lax.ppermute(x, AXES, route)

    def exchange(x):
        return lax.all_to_all(x, "seq", 0, 0, axis_index_groups=lines)

    flip, range_index, head = flip.reshape(1), range_index.reshape(1), head.reshape(1)
    keys, queries = pack(flip, teacher_key[0], student_key[0], teacher_query[0], student_query[0])
    own = exchange(keys)
    last = move(own, to_next)
    parting = own[1:]
    before = cross = move(parting, to_second)
    if relay:
        cross = move(move(parting, relay), to_cross)
    crossed = (seq_index // RING == seq // RING // 2) & (len(relay) > 0)
    keys = layout(crossed.astype(jnp.int32).reshape(1), own, last, before, cross)
    start, low = starts(range_index, segment_ids)
    queries = exchange(queries)
    dq, dk_own, dk_last, dk_before = attend(head, low, head_weight, start, queries, *keys)

    back_last = move(dk_last, reverse(to_next)).astype(F32)
    back_before = move(dk_before, reverse(to_second_straight)).astype(F32)
    dq_home = exchange(dq)
    total = dk_own + back_last + jnp.pad(back_before, ((1, 0), (0, 0), (0, 0)))
    query_grad, key_grad = unpack(flip, dq_home, exchange(total.astype(BF16)))
    return query_grad[None], key_grad[None]


def solution(mesh):
    seq, dp = mesh.shape["seq"], mesh.shape["dp"]
    spec = P("dp", "seq", None)
    return jax.shard_map(
        functools.partial(per_device, seq, dp),
        mesh=mesh,
        in_specs=(spec, spec, spec, spec, P("dp", None), P()),
        out_specs=(spec, spec),
        check_vma=False,
    )
```

```python
import functools
import math

import jax
import jax.numpy as jnp
from jax import lax
from jax.experimental import pallas as pl
from jax.experimental.pallas import tpu as pltpu
from jax.sharding import PartitionSpec as P

HEADS = 4
DIM = 128
TOK = 256
LINE = 4
RING = 8
BEHIND = 7
BAND = 12
OWN = 8
PAIR = 2 * TOK
MASKED = -1e30
F32 = jnp.float32
BF16 = jnp.bfloat16
VMEM = pl.BlockSpec(memory_space=pltpu.VMEM)
SMEM = pl.BlockSpec(memory_space=pltpu.SMEM)
AXES = ("seq", "dp")


def routes(seq, dp):
    rings = seq // RING
    last, before_last = [], []
    for ring in range(rings):
        for y in range(RING):
            for part in range(dp):
                me = (ring * RING + y) * dp + part
                ahead = ring + (y >= LINE)
                if ahead < rings:
                    last.append((me, (ahead * RING + RING - 1 - y) * dp + part))
                if ring + 1 < rings:
                    before_last.append((me, me + RING * dp))
    return last, before_last


def reverse(route):
    return [(b, a) for a, b in route]


def head_columns(flip, place):
    head = jnp.where(flip == 1, HEADS - 1 - place, place)
    return pl.ds(pl.multiple_of(head * DIM, DIM), DIM)


def pack_kernel(flip_ref, a_ref, b_ref, c_ref, d_ref, halo_ref, all_ref):
    for place in range(HEADS):
        columns = head_columns(1 - flip_ref[0], place)
        halo_ref[place, 0] = a_ref[:, columns]
        halo_ref[place, 1] = b_ref[:, columns]
    for place in range(HEADS):
        columns = head_columns(flip_ref[0], place)
        for i, ref in enumerate((a_ref, b_ref, c_ref, d_ref)):
            all_ref[place, i] = ref[:, columns]


def pack(flip, *states):
    return pl.pallas_call(
        pack_kernel,
        out_shape=[
            jax.ShapeDtypeStruct((HEADS, 2, TOK, DIM), BF16),
            jax.ShapeDtypeStruct((HEADS, 4, TOK, DIM), BF16),
        ],
        in_specs=[SMEM] + [VMEM] * 4,
        out_specs=[VMEM] * 2,
        cost_estimate=pl.CostEstimate(flops=0, bytes_accessed=2**21, transcendentals=0),
    )(flip, *states)


def starts_kernel(range_ref, seg_ref, start_ref, low_ref):
    first_block = range_ref[0] * LINE

    def ids(block):
        return seg_ref[0:1, pl.ds(pl.multiple_of(block * TOK, TOK), TOK)]

    own = [ids(first_block + j) for j in range(LINE)]
    ahead = [(first_block - b, ids(jnp.maximum(first_block - b, 0))) for b in range(1, BEHIND + 1)]
    counts = []
    for j in range(LINE):
        first = own[j][:, :1]
        same = jnp.zeros((1, TOK), jnp.int32)
        for i in range(j):
            same += (own[i] == first).astype(jnp.int32)
        for block, row in ahead[: BEHIND - j]:
            same += ((row == first) & (block >= 0)).astype(jnp.int32)
        counts.append(same)
    count = jnp.sum(jnp.concatenate(counts, axis=0), axis=1, keepdims=True)
    seg = jnp.concatenate(own, axis=0)
    column = lax.broadcasted_iota(jnp.int32, (LINE, TOK), 1)
    begin = jnp.where(seg != pltpu.roll(seg, 1, 1), column, 0)
    begin = jnp.where(column == 0, 0, begin)
    step = 1
    while step < TOK:
        begin = jnp.maximum(begin, jnp.where(column >= step, pltpu.roll(begin, step, 1), 0))
        step *= 2
    block_at = (OWN + lax.broadcasted_iota(jnp.int32, (LINE, TOK), 0)) * TOK
    start = block_at + jnp.where(begin > 0, begin, -count)
    start_ref[...] = start
    for j in range(LINE):
        low_ref[j] = jnp.min(start[j : j + 1, :])


def starts(range_index, seg):
    return pl.pallas_call(
        starts_kernel,
        out_shape=[jax.ShapeDtypeStruct((LINE, TOK), jnp.int32), jax.ShapeDtypeStruct((LINE,), jnp.int32)],
        in_specs=[SMEM, VMEM],
        out_specs=[VMEM, SMEM],
        cost_estimate=pl.CostEstimate(flops=0, bytes_accessed=2**20, transcendentals=0),
    )(range_index, seg)


def unpack_kernel(flip_ref, dq_ref, dk_ref, query_ref, key_ref):
    for place in range(HEADS):
        columns = head_columns(flip_ref[0], place)
        query_ref[:, columns] = dq_ref[place].astype(F32)
        key_ref[:, columns] = dk_ref[place].astype(F32)


def unpack(flip, dq, dk):
    return pl.pallas_call(
        unpack_kernel,
        out_shape=[jax.ShapeDtypeStruct((TOK, HEADS * DIM), F32)] * 2,
        in_specs=[SMEM, VMEM, VMEM],
        out_specs=[VMEM] * 2,
        cost_estimate=pl.CostEstimate(flops=0, bytes_accessed=12 * TOK * 512, transcendentals=0),
    )(flip, dq, dk)


def main_kernel(
    head_ref, low_ref, weight_ref, start_ref, all_ref, last_ref, before_ref,
    dq_ref, dk_own_ref, dk_last_ref, dk_before_ref,
    kt, ks, ks_turned, dk, et, es, top_t, top_s, dq_acc,
):
    weight = weight_ref[head_ref[0]]
    scale = 1.0 / math.sqrt(DIM)
    pace = scale * math.log2(math.e)
    along_depth = (((1,), (1,)), ((), ()))

    def rows(block):
        return pl.ds(block * TOK, TOK)

    lowest = low_ref[0] // TOK

    def load(block, teacher, student):
        kt[rows(block), :] = teacher
        ks[rows(block), :] = student
        ks_turned[:, rows(block)] = student.T
        dk[rows(block), :] = jnp.zeros((TOK, DIM), F32)

    def clear(block):
        load(block, jnp.zeros((TOK, DIM), BF16), jnp.zeros((TOK, DIM), BF16))

    for i in range(LINE):
        load(OWN + i, all_ref[i, 0], all_ref[i, 1])

    @pl.when(lowest <= OWN)
    def _():
        for i in range(LINE):
            load(LINE + i, last_ref[LINE - 1 - i, 0], last_ref[LINE - 1 - i, 1])

    @pl.when(lowest > OWN)
    def _():
        for i in range(LINE):
            clear(LINE + i)

    @pl.when(lowest <= LINE)
    def _():
        for i in range(LINE - 1):
            load(1 + i, before_ref[i, 0], before_ref[i, 1])

    @pl.when(lowest > LINE)
    def _():
        for i in range(LINE - 1):
            clear(1 + i)

    key_row = lax.broadcasted_iota(jnp.int32, (PAIR, TOK), 0)
    query_column = lax.broadcasted_iota(jnp.int32, (PAIR, TOK), 1)

    for j in range(LINE):
        block = OWN + j
        pairs = (block + 2 - low_ref[j] // TOK) // 2
        q_t, q_s = all_ref[j, 2], all_ref[j, 3]
        start = start_ref[j : j + 1, :]

        def at(t):
            return pl.multiple_of((block - 1 - 2 * t) * TOK, TOK)

        def one(keys, queries, visible, t, top, total, top_out, out):
            s = lax.dot_general(keys, queries, along_depth, preferred_element_type=F32)
            s = jnp.where(visible, s, MASKED)
            new_top = jnp.maximum(top, jnp.max(s, axis=0, keepdims=True))
            e = jnp.exp2((s - new_top) * pace)
            out[t] = e
            top_out[t] = new_top
            return new_top, total * jnp.exp2((top - new_top) * pace) + jnp.sum(e, axis=0, keepdims=True)

        def score(t, visible, carry):
            m_t, l_t, m_s, l_s = carry
            here = pl.ds(at(t), PAIR)
            m_t, l_t = one(kt[here, :], q_t, visible, t, m_t, l_t, top_t, et)
            m_s, l_s = one(ks[here, :], q_s, visible, t, m_s, l_s, top_s, es)
            return m_t, l_t, m_s, l_s

        def score_before(t, carry):
            return score(t, key_row >= start - at(t), carry)

        none, zero = jnp.full((1, TOK), MASKED, F32), jnp.zeros((1, TOK), F32)
        own_visible = (key_row <= query_column + TOK) & (key_row >= start - at(0))
        carry = score(0, own_visible, (none, zero, none, zero))
        m_t, l_t, m_s, l_s = lax.fori_loop(1, pairs, score_before, carry)
        r_t, r_s = weight / l_t, weight / l_s
        dq_acc[...] = jnp.zeros((DIM, TOK), F32)

        def grads(t, _):
            here = pl.ds(at(t), PAIR)
            f_t = jnp.exp2((top_t[t] - m_t) * pace) * r_t
            f_s = jnp.exp2((top_s[t] - m_s) * pace) * r_s
            grad = (es[t] * f_s - et[t] * f_t).astype(BF16)
            dk[here, :] += jnp.dot(grad, q_s, preferred_element_type=F32)
            dq_acc[...] += jnp.dot(ks_turned[:, here], grad, preferred_element_type=F32)
            return 0

        lax.fori_loop(0, pairs, grads, 0)
        dq_ref[j] = (dq_acc[...] * scale).T.astype(BF16)

    for i in range(LINE):
        dk_own_ref[i] = dk[rows(OWN + i), :] * scale
        dk_last_ref[i] = (dk[rows(LINE + i), :] * scale).astype(BF16)
    for i in range(LINE - 1):
        dk_before_ref[i] = (dk[rows(1 + i), :] * scale).astype(BF16)


def attend(head, low, weight, start, *states):
    return pl.pallas_call(
        main_kernel,
        out_shape=[
            jax.ShapeDtypeStruct((LINE, TOK, DIM), BF16),
            jax.ShapeDtypeStruct((LINE, TOK, DIM), F32),
            jax.ShapeDtypeStruct((LINE, TOK, DIM), BF16),
            jax.ShapeDtypeStruct((LINE - 1, TOK, DIM), BF16),
        ],
        in_specs=[SMEM] * 3 + [VMEM] * 4,
        out_specs=[VMEM] * 4,
        scratch_shapes=[
            pltpu.VMEM((BAND * TOK, DIM), BF16),
            pltpu.VMEM((BAND * TOK, DIM), BF16),
            pltpu.VMEM((DIM, BAND * TOK), BF16),
            pltpu.VMEM((BAND * TOK, DIM), F32),
            pltpu.VMEM((LINE, PAIR, TOK), F32),
            pltpu.VMEM((LINE, PAIR, TOK), F32),
            pltpu.VMEM((LINE, 1, TOK), F32),
            pltpu.VMEM((LINE, 1, TOK), F32),
            pltpu.VMEM((DIM, TOK), F32),
        ],
        compiler_params=pltpu.CompilerParams(vmem_limit_bytes=14 * 1024 * 1024),
        cost_estimate=pl.CostEstimate(flops=10**9, bytes_accessed=6 * 2**20, transcendentals=4 * 10**6),
    )(head, low, weight, start, *states)


def per_device(seq, dp, teacher_query, teacher_key, student_query, student_key, segment_ids, head_weight):
    to_next, to_second = routes(seq, dp)
    lines = [list(range(i, i + LINE)) for i in range(0, seq, LINE)]
    seq_index = lax.axis_index("seq")
    range_index = seq_index // LINE
    flip = lax.rem(range_index, 2)
    place = lax.rem(seq_index, LINE)
    head = jnp.where(flip == 1, HEADS - 1 - place, place)

    def move(x, route):
        return lax.ppermute(x, AXES, route)

    def exchange(x):
        return lax.all_to_all(x, "seq", 0, 0, axis_index_groups=lines)

    flip, range_index, head = flip.reshape(1), range_index.reshape(1), head.reshape(1)
    halo, states = pack(flip, teacher_key[0], student_key[0], teacher_query[0], student_query[0])
    halo = move(halo, to_next)
    states = exchange(states)
    before = move(states[1:, :2], to_second)
    last = exchange(halo)
    start, low = starts(range_index, segment_ids)
    dq, dk_own, dk_last, dk_before = attend(head, low, head_weight, start, states, last, before)

    back_last = move(dk_last, reverse(to_next)).astype(F32)
    back_before = move(dk_before, reverse(to_second)).astype(F32)
    dq_home = exchange(dq)
    total = dk_own + back_last + jnp.pad(back_before, ((1, 0), (0, 0), (0, 0)))
    query_grad, key_grad = unpack(flip, dq_home, exchange(total.astype(BF16)))
    return query_grad[None], key_grad[None]


def solution(mesh):
    seq, dp = mesh.shape["seq"], mesh.shape["dp"]
    spec = P("dp", "seq", None)
    return jax.shard_map(
        functools.partial(per_device, seq, dp),
        mesh=mesh,
        in_specs=(spec, spec, spec, spec, P("dp", None), P()),
        out_specs=(spec, spec),
        check_vma=False,
    )
```

```python
import functools
import math

import jax
import jax.numpy as jnp
from jax import lax
from jax.experimental import pallas as pl
from jax.experimental.pallas import tpu as pltpu
from jax.sharding import PartitionSpec as P

HEADS = 4
DIM = 128
TOK = 256
LINE = 4
RING = 8
BEHIND = 7
BAND = 12
OWN = 8
MASKED = -1e30
F32 = jnp.float32
BF16 = jnp.bfloat16
VMEM = pl.BlockSpec(memory_space=pltpu.VMEM)
SMEM = pl.BlockSpec(memory_space=pltpu.SMEM)
AXES = ("seq", "dp")


def routes(seq, dp):
    rings = seq // RING
    last, before_last = [], []
    for ring in range(rings):
        for y in range(RING):
            for part in range(dp):
                me = (ring * RING + y) * dp + part
                ahead = ring + (y >= LINE)
                if ahead < rings:
                    last.append((me, (ahead * RING + RING - 1 - y) * dp + part))
                if ring + 1 < rings:
                    before_last.append((me, me + RING * dp))
    return last, before_last


def reverse(route):
    return [(b, a) for a, b in route]


def head_columns(flip, place):
    head = jnp.where(flip == 1, HEADS - 1 - place, place)
    return pl.ds(pl.multiple_of(head * DIM, DIM), DIM)


def pack_kernel(flip_ref, a_ref, b_ref, c_ref, d_ref, keys_ref, queries_ref):
    for place in range(HEADS):
        columns = head_columns(flip_ref[0], place)
        keys_ref[place, 0] = a_ref[:, columns]
        keys_ref[place, 1] = b_ref[:, columns]
        queries_ref[place, 0] = c_ref[:, columns]
        queries_ref[place, 1] = d_ref[:, columns]


def pack(flip, *states):
    return pl.pallas_call(
        pack_kernel,
        out_shape=[jax.ShapeDtypeStruct((HEADS, 2, TOK, DIM), BF16)] * 2,
        in_specs=[SMEM] + [VMEM] * 4,
        out_specs=[VMEM] * 2,
        cost_estimate=pl.CostEstimate(flops=0, bytes_accessed=2**21, transcendentals=0),
    )(flip, *states)


def starts_kernel(range_ref, seg_ref, start_ref, low_ref):
    first_block = range_ref[0] * LINE

    def ids(block):
        return seg_ref[0:1, pl.ds(pl.multiple_of(block * TOK, TOK), TOK)]

    own = [ids(first_block + j) for j in range(LINE)]
    ahead = [(first_block - b, ids(jnp.maximum(first_block - b, 0))) for b in range(1, BEHIND + 1)]
    counts = []
    for j in range(LINE):
        first = own[j][:, :1]
        same = jnp.zeros((1, TOK), jnp.int32)
        for i in range(j):
            same += (own[i] == first).astype(jnp.int32)
        for block, row in ahead[: BEHIND - j]:
            same += ((row == first) & (block >= 0)).astype(jnp.int32)
        counts.append(same)
    count = jnp.sum(jnp.concatenate(counts, axis=0), axis=1, keepdims=True)
    seg = jnp.concatenate(own, axis=0)
    column = lax.broadcasted_iota(jnp.int32, (LINE, TOK), 1)
    begin = jnp.where(seg != pltpu.roll(seg, 1, 1), column, 0)
    begin = jnp.where(column == 0, 0, begin)
    step = 1
    while step < TOK:
        begin = jnp.maximum(begin, jnp.where(column >= step, pltpu.roll(begin, step, 1), 0))
        step *= 2
    block_at = (OWN + lax.broadcasted_iota(jnp.int32, (LINE, TOK), 0)) * TOK
    start = block_at + jnp.where(begin > 0, begin, -count)
    start_ref[...] = start
    for j in range(LINE):
        low_ref[j] = jnp.min(start[j : j + 1, :])


def starts(range_index, seg):
    return pl.pallas_call(
        starts_kernel,
        out_shape=[jax.ShapeDtypeStruct((LINE, TOK), jnp.int32), jax.ShapeDtypeStruct((LINE,), jnp.int32)],
        in_specs=[SMEM, VMEM],
        out_specs=[VMEM, SMEM],
        cost_estimate=pl.CostEstimate(flops=0, bytes_accessed=2**20, transcendentals=0),
    )(range_index, seg)


def unpack_kernel(flip_ref, dq_ref, dk_ref, query_ref, key_ref):
    for place in range(HEADS):
        columns = head_columns(flip_ref[0], place)
        query_ref[:, columns] = dq_ref[place].astype(F32)
        key_ref[:, columns] = dk_ref[place].astype(F32)


def unpack(flip, dq, dk):
    return pl.pallas_call(
        unpack_kernel,
        out_shape=[jax.ShapeDtypeStruct((TOK, HEADS * DIM), F32)] * 2,
        in_specs=[SMEM, VMEM, VMEM],
        out_specs=[VMEM] * 2,
        cost_estimate=pl.CostEstimate(flops=0, bytes_accessed=12 * TOK * 512, transcendentals=0),
    )(flip, dq, dk)


def layout_kernel(own_ref, last_ref, before_ref, kt, ks):
    def load(block, teacher, student):
        here = pl.ds(block * TOK, TOK)
        kt[here, :] = teacher
        ks[here, :] = student

    load(0, jnp.zeros((TOK, DIM), BF16), jnp.zeros((TOK, DIM), BF16))
    for i in range(LINE - 1):
        load(1 + i, before_ref[i, 0], before_ref[i, 1])
    for i in range(LINE):
        load(LINE + i, last_ref[i, 0], last_ref[i, 1])
        load(OWN + i, own_ref[i, 0], own_ref[i, 1])


def layout(own, last, before):
    return pl.pallas_call(
        layout_kernel,
        out_shape=[
            jax.ShapeDtypeStruct((BAND * TOK, DIM), BF16),
            jax.ShapeDtypeStruct((BAND * TOK, DIM), BF16),
        ],
        in_specs=[VMEM] * 3,
        out_specs=[VMEM] * 2,
        compiler_params=pltpu.CompilerParams(vmem_limit_bytes=6 * 1024 * 1024),
        cost_estimate=pl.CostEstimate(flops=10**10, bytes_accessed=16 * 2**20, transcendentals=0),
    )(own, last, before)


def main_kernel(
    head_ref, low_ref, weight_ref, start_ref, query_ref, kt, ks,
    dq_ref, dk_own_ref, dk_last_ref, dk_before_ref,
    ks_turned, dk, et, es, grad,
):
    weight = weight_ref[head_ref[0]]
    scale = 1.0 / math.sqrt(DIM)
    pace = scale * math.log2(math.e)
    along_depth = (((1,), (1,)), ((), ()))
    lowest = low_ref[0] // TOK

    def rows(block):
        return pl.ds(block * TOK, TOK)

    dk[...] = jnp.zeros((BAND * TOK, DIM), F32)
    for block in range(BAND):
        @pl.when(block >= lowest - 1)
        def _():
            ks_turned[:, rows(block)] = ks[rows(block), :].T

    def work(j, blocks):
        base = pl.multiple_of((OWN + j + 1 - blocks) * TOK, TOK)
        q_t, q_s = query_ref[j, 0], query_ref[j, 1]
        start = start_ref[pl.ds(j, 1), :] - base
        key_row = lax.broadcasted_iota(jnp.int32, (TOK, TOK), 0)
        causal = key_row <= lax.broadcasted_iota(jnp.int32, (TOK, TOK), 1)

        def keys(i):
            return pl.ds(pl.multiple_of(base + i * TOK, TOK), TOK)

        m_t = m_s = None
        for i in range(blocks):
            visible = key_row >= start - i * TOK
            if i == blocks - 1:
                visible = visible & causal
            s_t = lax.dot_general(kt[keys(i), :], q_t, along_depth, preferred_element_type=F32)
            s_s = lax.dot_general(ks[keys(i), :], q_s, along_depth, preferred_element_type=F32)
            s_t = jnp.where(visible, s_t, MASKED)
            s_s = jnp.where(visible, s_s, MASKED)
            et[i] = s_t
            es[i] = s_s
            h_t, h_s = jnp.max(s_t, axis=0, keepdims=True), jnp.max(s_s, axis=0, keepdims=True)
            m_t = h_t if m_t is None else jnp.maximum(m_t, h_t)
            m_s = h_s if m_s is None else jnp.maximum(m_s, h_s)
        l_t = l_s = jnp.zeros((1, TOK), F32)
        for i in range(blocks):
            e_t = jnp.exp2((et[i] - m_t) * pace)
            e_s = jnp.exp2((es[i] - m_s) * pace)
            et[i] = e_t
            es[i] = e_s
            l_t += jnp.sum(e_t, axis=0, keepdims=True)
            l_s += jnp.sum(e_s, axis=0, keepdims=True)
        r_t, r_s = weight / l_t, weight / l_s
        for i in range(blocks):
            g = (es[i] * r_s - et[i] * r_t).astype(BF16)
            grad[rows(i), :] = g
            dk[keys(i), :] += jnp.dot(g, q_s, preferred_element_type=F32)
        dq = jnp.dot(
            ks_turned[:, pl.ds(base, blocks * TOK)], grad[: blocks * TOK, :], preferred_element_type=F32
        )
        dq_ref[j] = (dq * scale).T.astype(BF16)

    def query_block(j, _):
        pairs = (OWN + j + 2 - low_ref[j] // TOK) // 2
        for p in range(1, LINE + 1):
            @pl.when(pairs == p)
            def _():
                work(j, 2 * p)

        return 0

    lax.fori_loop(0, LINE, query_block, 0)

    for i in range(LINE):
        dk_own_ref[i] = dk[rows(OWN + i), :] * scale
        dk_last_ref[i] = (dk[rows(LINE + i), :] * scale).astype(BF16)
    for i in range(LINE - 1):
        dk_before_ref[i] = (dk[rows(1 + i), :] * scale).astype(BF16)


def attend(head, low, weight, start, queries, *keys):
    return pl.pallas_call(
        main_kernel,
        out_shape=[
            jax.ShapeDtypeStruct((LINE, TOK, DIM), BF16),
            jax.ShapeDtypeStruct((LINE, TOK, DIM), F32),
            jax.ShapeDtypeStruct((LINE, TOK, DIM), BF16),
            jax.ShapeDtypeStruct((LINE - 1, TOK, DIM), BF16),
        ],
        in_specs=[SMEM] * 3 + [VMEM] * 4,
        out_specs=[VMEM] * 4,
        scratch_shapes=[
            pltpu.VMEM((DIM, BAND * TOK), BF16),
            pltpu.VMEM((BAND * TOK, DIM), F32),
            pltpu.VMEM((OWN, TOK, TOK), F32),
            pltpu.VMEM((OWN, TOK, TOK), F32),
            pltpu.VMEM((OWN * TOK, TOK), BF16),
        ],
        compiler_params=pltpu.CompilerParams(vmem_limit_bytes=12 * 1024 * 1024),
        cost_estimate=pl.CostEstimate(flops=10**9, bytes_accessed=6 * 2**20, transcendentals=4 * 10**6),
    )(head, low, weight, start, queries, *keys)


def per_device(seq, dp, teacher_query, teacher_key, student_query, student_key, segment_ids, head_weight):
    to_next, to_second = routes(seq, dp)
    lines = [list(range(i, i + LINE)) for i in range(0, seq, LINE)]
    seq_index = lax.axis_index("seq")
    range_index = seq_index // LINE
    flip = lax.rem(range_index, 2)
    place = lax.rem(seq_index, LINE)
    head = jnp.where(flip == 1, HEADS - 1 - place, place)

    def move(x, route):
        return lax.ppermute(x, AXES, route)

    def exchange(x):
        return lax.all_to_all(x, "seq", 0, 0, axis_index_groups=lines)

    flip, range_index, head = flip.reshape(1), range_index.reshape(1), head.reshape(1)
    keys, queries = pack(flip, teacher_key[0], student_key[0], teacher_query[0], student_query[0])
    own = exchange(keys)
    last = move(own, to_next)
    before = move(own[1:], to_second)
    start, low = starts(range_index, segment_ids)
    queries = exchange(queries)
    dq, dk_own, dk_last, dk_before = attend(head, low, head_weight, start, queries, *layout(own, last, before))

    back_last = move(dk_last, reverse(to_next)).astype(F32)
    back_before = move(dk_before, reverse(to_second)).astype(F32)
    dq_home = exchange(dq)
    total = dk_own + back_last + jnp.pad(back_before, ((1, 0), (0, 0), (0, 0)))
    query_grad, key_grad = unpack(flip, dq_home, exchange(total.astype(BF16)))
    return query_grad[None], key_grad[None]


def solution(mesh):
    seq, dp = mesh.shape["seq"], mesh.shape["dp"]
    spec = P("dp", "seq", None)
    return jax.shard_map(
        functools.partial(per_device, seq, dp),
        mesh=mesh,
        in_specs=(spec, spec, spec, spec, P("dp", None), P()),
        out_specs=(spec, spec),
        check_vma=False,
    )
```

```python
import functools
import math

import jax
import jax.numpy as jnp
from jax import lax
from jax.experimental import pallas as pl
from jax.experimental.pallas import tpu as pltpu
from jax.sharding import PartitionSpec as P

HEADS = 4
DIM = 128
TOK = 256
LINE = 4
RING = 8
BEHIND = 7
BAND = 12
OWN = 8
PART = 64
MASKED = -1e30
F32 = jnp.float32
BF16 = jnp.bfloat16
VMEM = pl.BlockSpec(memory_space=pltpu.VMEM)
SMEM = pl.BlockSpec(memory_space=pltpu.SMEM)
AXES = ("seq", "dp")


def routes(seq, dp):
    rings = seq // RING
    last, before_last = [], []
    for ring in range(rings):
        for y in range(RING):
            for part in range(dp):
                me = (ring * RING + y) * dp + part
                ahead = ring + (y >= LINE)
                if ahead < rings:
                    last.append((me, (ahead * RING + RING - 1 - y) * dp + part))
                if ring + 1 < rings:
                    before_last.append((me, me + RING * dp))
    return last, before_last


def reverse(route):
    return [(b, a) for a, b in route]


def head_columns(flip, place):
    head = jnp.where(flip == 1, HEADS - 1 - place, place)
    return pl.ds(pl.multiple_of(head * DIM, DIM), DIM)


def pack_kernel(flip_ref, a_ref, b_ref, c_ref, d_ref, keys_ref, queries_ref):
    for place in range(HEADS):
        columns = head_columns(flip_ref[0], place)
        keys_ref[place, 0] = a_ref[:, columns]
        keys_ref[place, 1] = b_ref[:, columns]
        queries_ref[place, 0] = c_ref[:, columns]
        queries_ref[place, 1] = d_ref[:, columns]


def pack(flip, *states):
    return pl.pallas_call(
        pack_kernel,
        out_shape=[jax.ShapeDtypeStruct((HEADS, 2, TOK, DIM), BF16)] * 2,
        in_specs=[SMEM] + [VMEM] * 4,
        out_specs=[VMEM] * 2,
        cost_estimate=pl.CostEstimate(flops=0, bytes_accessed=2**21, transcendentals=0),
    )(flip, *states)


def starts_kernel(range_ref, seg_ref, start_ref, low_ref):
    first_block = range_ref[0] * LINE

    def ids(block):
        return seg_ref[0:1, pl.ds(pl.multiple_of(block * TOK, TOK), TOK)]

    own = [ids(first_block + j) for j in range(LINE)]
    ahead = [(first_block - b, ids(jnp.maximum(first_block - b, 0))) for b in range(1, BEHIND + 1)]
    counts = []
    for j in range(LINE):
        first = own[j][:, :1]
        same = jnp.zeros((1, TOK), jnp.int32)
        for i in range(j):
            same += (own[i] == first).astype(jnp.int32)
        for block, row in ahead[: BEHIND - j]:
            same += ((row == first) & (block >= 0)).astype(jnp.int32)
        counts.append(same)
    count = jnp.sum(jnp.concatenate(counts, axis=0), axis=1, keepdims=True)
    seg = jnp.concatenate(own, axis=0)
    column = lax.broadcasted_iota(jnp.int32, (LINE, TOK), 1)
    begin = jnp.where(seg != pltpu.roll(seg, 1, 1), column, 0)
    begin = jnp.where(column == 0, 0, begin)
    step = 1
    while step < TOK:
        begin = jnp.maximum(begin, jnp.where(column >= step, pltpu.roll(begin, step, 1), 0))
        step *= 2
    block_at = (OWN + lax.broadcasted_iota(jnp.int32, (LINE, TOK), 0)) * TOK
    start = block_at + jnp.where(begin > 0, begin, -count)
    start_ref[...] = start
    for j in range(LINE):
        low_ref[j] = jnp.min(start[j : j + 1, :])


def starts(range_index, seg):
    return pl.pallas_call(
        starts_kernel,
        out_shape=[jax.ShapeDtypeStruct((LINE, TOK), jnp.int32), jax.ShapeDtypeStruct((LINE,), jnp.int32)],
        in_specs=[SMEM, VMEM],
        out_specs=[VMEM, SMEM],
        cost_estimate=pl.CostEstimate(flops=0, bytes_accessed=2**20, transcendentals=0),
    )(range_index, seg)


def unpack_kernel(flip_ref, dq_ref, dk_ref, query_ref, key_ref):
    for place in range(HEADS):
        columns = head_columns(flip_ref[0], place)
        query_ref[:, columns] = dq_ref[place].astype(F32)
        key_ref[:, columns] = dk_ref[place].astype(F32)


def unpack(flip, dq, dk):
    return pl.pallas_call(
        unpack_kernel,
        out_shape=[jax.ShapeDtypeStruct((TOK, HEADS * DIM), F32)] * 2,
        in_specs=[SMEM, VMEM, VMEM],
        out_specs=[VMEM] * 2,
        cost_estimate=pl.CostEstimate(flops=0, bytes_accessed=12 * TOK * 512, transcendentals=0),
    )(flip, dq, dk)


def layout_kernel(own_ref, last_ref, before_ref, kt, ks):
    def load(block, teacher, student):
        here = pl.ds(block * TOK, TOK)
        kt[here, :] = teacher
        ks[here, :] = student

    load(0, jnp.zeros((TOK, DIM), BF16), jnp.zeros((TOK, DIM), BF16))
    for i in range(LINE - 1):
        load(1 + i, before_ref[i, 0], before_ref[i, 1])
    for i in range(LINE):
        load(LINE + i, last_ref[i, 0], last_ref[i, 1])
        load(OWN + i, own_ref[i, 0], own_ref[i, 1])


def layout(own, last, before):
    return pl.pallas_call(
        layout_kernel,
        out_shape=[
            jax.ShapeDtypeStruct((BAND * TOK, DIM), BF16),
            jax.ShapeDtypeStruct((BAND * TOK, DIM), BF16),
        ],
        in_specs=[VMEM] * 3,
        out_specs=[VMEM] * 2,
        compiler_params=pltpu.CompilerParams(vmem_limit_bytes=6 * 1024 * 1024),
        cost_estimate=pl.CostEstimate(flops=10**10, bytes_accessed=16 * 2**20, transcendentals=0),
    )(own, last, before)


def main_kernel(
    head_ref, low_ref, weight_ref, start_ref, query_ref, kt, ks,
    dq_ref, dk_own_ref, dk_last_ref, dk_before_ref,
    ks_turned, dk, et, es, grad, top_t, top_s, sum_t, sum_s, factor_t, factor_s,
):
    weight = weight_ref[head_ref[0]]
    scale = 1.0 / math.sqrt(DIM)
    pace = scale * math.log2(math.e)
    lowest = low_ref[0] // TOK

    def rows(block):
        return pl.ds(block * TOK, TOK)

    dk[...] = jnp.zeros((BAND * TOK, DIM), F32)
    for block in range(BAND):
        @pl.when(block >= lowest - 1)
        def _():
            ks_turned[:, rows(block)] = ks[rows(block), :].T

    def work(j, blocks):
        base = pl.multiple_of((OWN + j + 1 - blocks) * TOK, TOK)
        q_t, q_s = query_ref[j, 0], query_ref[j, 1]
        sides = (
            (kt, q_t.T, et, top_t, sum_t, factor_t),
            (ks, q_s.T, es, top_s, sum_s, factor_s),
        )
        start = start_ref[pl.ds(j, 1), :] - base
        key_row = lax.broadcasted_iota(jnp.int32, (PART, TOK), 0)
        query_column = lax.broadcasted_iota(jnp.int32, (PART, TOK), 1)
        parts = [(i, c) for i in range(blocks) for c in range(TOK // PART)]
        held = pl.ds(0, len(parts))

        def keys(i):
            return pl.ds(pl.multiple_of(base + i * TOK, TOK), TOK)

        for i in range(blocks):
            scores = [jnp.dot(k[keys(i), :], q, preferred_element_type=F32) for k, q, *_ in sides]
            for c in range(TOK // PART):
                here, at = pl.ds(c * PART, PART), i * (TOK // PART) + c
                visible = key_row >= start - (i * TOK + c * PART)
                if i == blocks - 1:
                    visible = visible & (key_row <= query_column - c * PART)
                for s, (_, _, e, top, total, _) in zip(scores, sides):
                    x = jnp.where(visible, s[c * PART : (c + 1) * PART], MASKED)
                    h = jnp.max(x, axis=0, keepdims=True)
                    x = jnp.exp2((x - h) * pace)
                    e[i, here, :] = x
                    top[pl.ds(at, 1), :] = h
                    total[pl.ds(at, 1), :] = jnp.sum(x, axis=0, keepdims=True)
        for _, _, _, top, total, factor in sides:
            tops = top[held, :]
            f = jnp.exp2((tops - jnp.max(tops, axis=0, keepdims=True)) * pace)
            factor[held, :] = f * (weight / jnp.sum(total[held, :] * f, axis=0, keepdims=True))
        for i in range(blocks):
            for c in range(TOK // PART):
                here, at = pl.ds(c * PART, PART), pl.ds(i * (TOK // PART) + c, 1)
                g = es[i, here, :] * factor_s[at, :] - et[i, here, :] * factor_t[at, :]
                grad[pl.ds(i * TOK + c * PART, PART), :] = g.astype(BF16)
            dk[keys(i), :] += jnp.dot(grad[rows(i), :], q_s, preferred_element_type=F32)
        dq = jnp.dot(
            ks_turned[:, pl.ds(base, blocks * TOK)], grad[: blocks * TOK, :], preferred_element_type=F32
        )
        dq_ref[j] = (dq * scale).T.astype(BF16)

    def query_block(j, _):
        pairs = (OWN + j + 2 - low_ref[j] // TOK) // 2
        for p in range(1, LINE + 1):
            @pl.when(pairs == p)
            def _():
                work(j, 2 * p)

        return 0

    lax.fori_loop(0, LINE, query_block, 0)

    for i in range(LINE):
        dk_own_ref[i] = dk[rows(OWN + i), :] * scale
        dk_last_ref[i] = (dk[rows(LINE + i), :] * scale).astype(BF16)
    for i in range(LINE - 1):
        dk_before_ref[i] = (dk[rows(1 + i), :] * scale).astype(BF16)


def attend(head, low, weight, start, queries, *keys):
    return pl.pallas_call(
        main_kernel,
        out_shape=[
            jax.ShapeDtypeStruct((LINE, TOK, DIM), BF16),
            jax.ShapeDtypeStruct((LINE, TOK, DIM), F32),
            jax.ShapeDtypeStruct((LINE, TOK, DIM), BF16),
            jax.ShapeDtypeStruct((LINE - 1, TOK, DIM), BF16),
        ],
        in_specs=[SMEM] * 3 + [VMEM] * 4,
        out_specs=[VMEM] * 4,
        scratch_shapes=[
            pltpu.VMEM((DIM, BAND * TOK), BF16),
            pltpu.VMEM((BAND * TOK, DIM), F32),
            pltpu.VMEM((OWN, TOK, TOK), F32),
            pltpu.VMEM((OWN, TOK, TOK), F32),
            pltpu.VMEM((OWN * TOK, TOK), BF16),
        ]
        + [pltpu.VMEM((OWN * TOK // PART, TOK), F32)] * 6,
        compiler_params=pltpu.CompilerParams(vmem_limit_bytes=12 * 1024 * 1024),
        cost_estimate=pl.CostEstimate(flops=10**9, bytes_accessed=6 * 2**20, transcendentals=4 * 10**6),
    )(head, low, weight, start, queries, *keys)


def per_device(seq, dp, teacher_query, teacher_key, student_query, student_key, segment_ids, head_weight):
    to_next, to_second = routes(seq, dp)
    lines = [list(range(i, i + LINE)) for i in range(0, seq, LINE)]
    seq_index = lax.axis_index("seq")
    range_index = seq_index // LINE
    flip = lax.rem(range_index, 2)
    place = lax.rem(seq_index, LINE)
    head = jnp.where(flip == 1, HEADS - 1 - place, place)

    def move(x, route):
        return lax.ppermute(x, AXES, route)

    def exchange(x):
        return lax.all_to_all(x, "seq", 0, 0, axis_index_groups=lines)

    flip, range_index, head = flip.reshape(1), range_index.reshape(1), head.reshape(1)
    keys, queries = pack(flip, teacher_key[0], student_key[0], teacher_query[0], student_query[0])
    own = exchange(keys)
    last = move(own, to_next)
    before = move(own[1:], to_second)
    start, low = starts(range_index, segment_ids)
    queries = exchange(queries)
    dq, dk_own, dk_last, dk_before = attend(head, low, head_weight, start, queries, *layout(own, last, before))

    back_last = move(dk_last, reverse(to_next)).astype(F32)
    back_before = move(dk_before, reverse(to_second)).astype(F32)
    dq_home = exchange(dq)
    total = dk_own + back_last + jnp.pad(back_before, ((1, 0), (0, 0), (0, 0)))
    query_grad, key_grad = unpack(flip, dq_home, exchange(total.astype(BF16)))
    return query_grad[None], key_grad[None]


def solution(mesh):
    seq, dp = mesh.shape["seq"], mesh.shape["dp"]
    spec = P("dp", "seq", None)
    return jax.shard_map(
        functools.partial(per_device, seq, dp),
        mesh=mesh,
        in_specs=(spec, spec, spec, spec, P("dp", None), P()),
        out_specs=(spec, spec),
        check_vma=False,
    )
```

```python
import functools
import math

import jax
import jax.numpy as jnp
from jax import lax
from jax.experimental import pallas as pl
from jax.experimental.pallas import tpu as pltpu
from jax.sharding import PartitionSpec as P

HEADS = 4
DIM = 128
TOK = 256
LINE = 4
RING = 8
BEHIND = 7
BAND = 12
OWN = 8
PART = 64
WIDE = 2 * TOK
SPAN = 10
MASKED = -1e30
F32 = jnp.float32
BF16 = jnp.bfloat16
VMEM = pl.BlockSpec(memory_space=pltpu.VMEM)
SMEM = pl.BlockSpec(memory_space=pltpu.SMEM)
AXES = ("seq", "dp")


def routes(seq, dp):
    rings = seq // RING
    last, before_last = [], []
    for ring in range(rings):
        for y in range(RING):
            for part in range(dp):
                me = (ring * RING + y) * dp + part
                ahead = ring + (y >= LINE)
                if ahead < rings:
                    last.append((me, (ahead * RING + RING - 1 - y) * dp + part))
                if ring + 1 < rings:
                    before_last.append((me, me + RING * dp))
    return last, before_last


def reverse(route):
    return [(b, a) for a, b in route]


def head_columns(flip, place):
    head = jnp.where(flip == 1, HEADS - 1 - place, place)
    return pl.ds(pl.multiple_of(head * DIM, DIM), DIM)


def pack_kernel(flip_ref, a_ref, b_ref, c_ref, d_ref, keys_ref, queries_ref):
    for place in range(HEADS):
        columns = head_columns(flip_ref[0], place)
        keys_ref[place, 0] = a_ref[:, columns]
        keys_ref[place, 1] = b_ref[:, columns]
        queries_ref[place, 0] = c_ref[:, columns]
        queries_ref[place, 1] = d_ref[:, columns]


def pack(flip, *states):
    return pl.pallas_call(
        pack_kernel,
        out_shape=[jax.ShapeDtypeStruct((HEADS, 2, TOK, DIM), BF16)] * 2,
        in_specs=[SMEM] + [VMEM] * 4,
        out_specs=[VMEM] * 2,
        cost_estimate=pl.CostEstimate(flops=0, bytes_accessed=2**21, transcendentals=0),
    )(flip, *states)


def starts_kernel(range_ref, seg_ref, start_ref, low_ref):
    first_block = range_ref[0] * LINE

    def ids(block):
        return seg_ref[0:1, pl.ds(pl.multiple_of(block * TOK, TOK), TOK)]

    own = [ids(first_block + j) for j in range(LINE)]
    ahead = [(first_block - b, ids(jnp.maximum(first_block - b, 0))) for b in range(1, BEHIND + 1)]
    counts = []
    for j in range(LINE):
        first = own[j][:, :1]
        same = jnp.zeros((1, TOK), jnp.int32)
        for i in range(j):
            same += (own[i] == first).astype(jnp.int32)
        for block, row in ahead[: BEHIND - j]:
            same += ((row == first) & (block >= 0)).astype(jnp.int32)
        counts.append(same)
    count = jnp.sum(jnp.concatenate(counts, axis=0), axis=1, keepdims=True)
    seg = jnp.concatenate(own, axis=0)
    column = lax.broadcasted_iota(jnp.int32, (LINE, TOK), 1)
    begin = jnp.where(seg != pltpu.roll(seg, 1, 1), column, 0)
    begin = jnp.where(column == 0, 0, begin)
    step = 1
    while step < TOK:
        begin = jnp.maximum(begin, jnp.where(column >= step, pltpu.roll(begin, step, 1), 0))
        step *= 2
    block_at = (OWN + lax.broadcasted_iota(jnp.int32, (LINE, TOK), 0)) * TOK
    start = block_at + jnp.where(begin > 0, begin, -count)
    start_ref[...] = start
    for j in range(LINE):
        low_ref[j] = jnp.min(start[j : j + 1, :])


def starts(range_index, seg):
    return pl.pallas_call(
        starts_kernel,
        out_shape=[jax.ShapeDtypeStruct((LINE, TOK), jnp.int32), jax.ShapeDtypeStruct((LINE,), jnp.int32)],
        in_specs=[SMEM, VMEM],
        out_specs=[VMEM, SMEM],
        cost_estimate=pl.CostEstimate(flops=0, bytes_accessed=2**20, transcendentals=0),
    )(range_index, seg)


def unpack_kernel(flip_ref, dq_ref, dk_ref, query_ref, key_ref):
    for place in range(HEADS):
        columns = head_columns(flip_ref[0], place)
        query_ref[:, columns] = dq_ref[place].astype(F32)
        key_ref[:, columns] = dk_ref[place].astype(F32)


def unpack(flip, dq, dk):
    return pl.pallas_call(
        unpack_kernel,
        out_shape=[jax.ShapeDtypeStruct((TOK, HEADS * DIM), F32)] * 2,
        in_specs=[SMEM, VMEM, VMEM],
        out_specs=[VMEM] * 2,
        cost_estimate=pl.CostEstimate(flops=0, bytes_accessed=12 * TOK * 512, transcendentals=0),
    )(flip, dq, dk)


def layout_kernel(own_ref, last_ref, before_ref, kt, ks):
    def load(block, teacher, student):
        here = pl.ds(block * TOK, TOK)
        kt[here, :] = teacher
        ks[here, :] = student

    load(0, jnp.zeros((TOK, DIM), BF16), jnp.zeros((TOK, DIM), BF16))
    for i in range(LINE - 1):
        load(1 + i, before_ref[i, 0], before_ref[i, 1])
    for i in range(LINE):
        load(LINE + i, last_ref[i, 0], last_ref[i, 1])
        load(OWN + i, own_ref[i, 0], own_ref[i, 1])


def layout(own, last, before):
    return pl.pallas_call(
        layout_kernel,
        out_shape=[
            jax.ShapeDtypeStruct((BAND * TOK, DIM), BF16),
            jax.ShapeDtypeStruct((BAND * TOK, DIM), BF16),
        ],
        in_specs=[VMEM] * 3,
        out_specs=[VMEM] * 2,
        compiler_params=pltpu.CompilerParams(vmem_limit_bytes=6 * 1024 * 1024),
        cost_estimate=pl.CostEstimate(flops=10**10, bytes_accessed=16 * 2**20, transcendentals=0),
    )(own, last, before)


def main_kernel(
    head_ref, low_ref, weight_ref, start_ref, query_ref, kt, ks,
    dq_ref, dk_own_ref, dk_last_ref, dk_before_ref,
    ks_turned, dk, et, es, grad, top_t, top_s, sum_t, sum_s, factor_t, factor_s,
):
    weight = weight_ref[head_ref[0]]
    scale = 1.0 / math.sqrt(DIM)
    pace = scale * math.log2(math.e)
    lowest = low_ref[0] // TOK

    def rows(block):
        return pl.ds(block * TOK, TOK)

    def turned(j, kind):
        return jnp.concatenate([query_ref[j, kind].T, query_ref[j + 1, kind].T], axis=1)

    dk[...] = jnp.zeros((BAND * TOK, DIM), F32)
    for block in range(BAND):
        @pl.when(block >= lowest - 1)
        def _():
            ks_turned[:, rows(block)] = ks[rows(block), :].T

    def work(j, blocks):
        base = pl.multiple_of((OWN + j + 2 - blocks) * TOK, TOK)
        sides = (
            (kt, turned(j, 0), et, top_t, sum_t, factor_t),
            (ks, turned(j, 1), es, top_s, sum_s, factor_s),
        )
        q_s = jnp.concatenate([query_ref[j, 1], query_ref[j + 1, 1]], axis=0)
        start = jnp.concatenate([start_ref[pl.ds(j, 1), :], start_ref[pl.ds(j + 1, 1), :]], axis=1) - base
        key_row = lax.broadcasted_iota(jnp.int32, (PART, WIDE), 0)
        query_column = lax.broadcasted_iota(jnp.int32, (PART, WIDE), 1)
        parts = [(i, c) for i in range(blocks) for c in range(TOK // PART)]
        held = pl.ds(0, len(parts))

        def keys(i):
            return pl.ds(pl.multiple_of(base + i * TOK, TOK), TOK)

        for i in range(blocks):
            scores = [jnp.dot(k[keys(i), :], q, preferred_element_type=F32) for k, q, *_ in sides]
            for c in range(TOK // PART):
                here, at = pl.ds(c * PART, PART), i * (TOK // PART) + c
                visible = key_row >= start - (i * TOK + c * PART)
                if i >= blocks - 2:
                    visible = visible & (key_row <= query_column - ((i - blocks + 2) * TOK + c * PART))
                for s, (_, _, e, top, total, _) in zip(scores, sides):
                    x = jnp.where(visible, s[c * PART : (c + 1) * PART], MASKED)
                    h = jnp.max(x, axis=0, keepdims=True)
                    x = jnp.exp2((x - h) * pace)
                    e[i, here, :] = x
                    top[pl.ds(at, 1), :] = h
                    total[pl.ds(at, 1), :] = jnp.sum(x, axis=0, keepdims=True)
        for _, _, _, top, total, factor in sides:
            tops = top[held, :]
            f = jnp.exp2((tops - jnp.max(tops, axis=0, keepdims=True)) * pace)
            factor[held, :] = f * (weight / jnp.sum(total[held, :] * f, axis=0, keepdims=True))
        for i in range(blocks):
            for c in range(TOK // PART):
                here, at = pl.ds(c * PART, PART), pl.ds(i * (TOK // PART) + c, 1)
                g = es[i, here, :] * factor_s[at, :] - et[i, here, :] * factor_t[at, :]
                grad[pl.ds(i * TOK + c * PART, PART), :] = g.astype(BF16)
            dk[keys(i), :] += jnp.dot(grad[rows(i), :], q_s, preferred_element_type=F32)
        dq = jnp.dot(
            ks_turned[:, pl.ds(base, blocks * TOK)], grad[: blocks * TOK, :], preferred_element_type=F32
        )
        dq_ref[j] = (dq[:, :TOK] * scale).T.astype(BF16)
        dq_ref[j + 1] = (dq[:, TOK:] * scale).T.astype(BF16)

    def query_blocks(step, _):
        j = 2 * step
        pairs = (OWN + j + 3 - low_ref[j] // TOK) // 2
        for p in range(1, SPAN // 2 + 1):
            @pl.when(pairs == p)
            def _():
                work(j, 2 * p)

        return 0

    lax.fori_loop(0, LINE // 2, query_blocks, 0)

    for i in range(LINE):
        dk_own_ref[i] = dk[rows(OWN + i), :] * scale
        dk_last_ref[i] = (dk[rows(LINE + i), :] * scale).astype(BF16)
    for i in range(LINE - 1):
        dk_before_ref[i] = (dk[rows(1 + i), :] * scale).astype(BF16)


def attend(head, low, weight, start, queries, *keys):
    return pl.pallas_call(
        main_kernel,
        out_shape=[
            jax.ShapeDtypeStruct((LINE, TOK, DIM), BF16),
            jax.ShapeDtypeStruct((LINE, TOK, DIM), F32),
            jax.ShapeDtypeStruct((LINE, TOK, DIM), BF16),
            jax.ShapeDtypeStruct((LINE - 1, TOK, DIM), BF16),
        ],
        in_specs=[SMEM] * 3 + [VMEM] * 4,
        out_specs=[VMEM] * 4,
        scratch_shapes=[
            pltpu.VMEM((DIM, BAND * TOK), BF16),
            pltpu.VMEM((BAND * TOK, DIM), F32),
            pltpu.VMEM((SPAN, TOK, WIDE), F32),
            pltpu.VMEM((SPAN, TOK, WIDE), F32),
            pltpu.VMEM((SPAN * TOK, WIDE), BF16),
        ]
        + [pltpu.VMEM((SPAN * TOK // PART, WIDE), F32)] * 6,
        compiler_params=pltpu.CompilerParams(vmem_limit_bytes=24 * 1024 * 1024),
        cost_estimate=pl.CostEstimate(flops=10**9, bytes_accessed=6 * 2**20, transcendentals=4 * 10**6),
    )(head, low, weight, start, queries, *keys)


def per_device(seq, dp, teacher_query, teacher_key, student_query, student_key, segment_ids, head_weight):
    to_next, to_second = routes(seq, dp)
    lines = [list(range(i, i + LINE)) for i in range(0, seq, LINE)]
    seq_index = lax.axis_index("seq")
    range_index = seq_index // LINE
    flip = lax.rem(range_index, 2)
    place = lax.rem(seq_index, LINE)
    head = jnp.where(flip == 1, HEADS - 1 - place, place)

    def move(x, route):
        return lax.ppermute(x, AXES, route)

    def exchange(x):
        return lax.all_to_all(x, "seq", 0, 0, axis_index_groups=lines)

    flip, range_index, head = flip.reshape(1), range_index.reshape(1), head.reshape(1)
    keys, queries = pack(flip, teacher_key[0], student_key[0], teacher_query[0], student_query[0])
    own = exchange(keys)
    last = move(own, to_next)
    before = move(own[1:], to_second)
    start, low = starts(range_index, segment_ids)
    queries = exchange(queries)
    dq, dk_own, dk_last, dk_before = attend(head, low, head_weight, start, queries, *layout(own, last, before))

    back_last = move(dk_last, reverse(to_next)).astype(F32)
    back_before = move(dk_before, reverse(to_second)).astype(F32)
    dq_home = exchange(dq)
    total = dk_own + back_last + jnp.pad(back_before, ((1, 0), (0, 0), (0, 0)))
    query_grad, key_grad = unpack(flip, dq_home, exchange(total.astype(BF16)))
    return query_grad[None], key_grad[None]


def solution(mesh):
    seq, dp = mesh.shape["seq"], mesh.shape["dp"]
    spec = P("dp", "seq", None)
    return jax.shard_map(
        functools.partial(per_device, seq, dp),
        mesh=mesh,
        in_specs=(spec, spec, spec, spec, P("dp", None), P()),
        out_specs=(spec, spec),
        check_vma=False,
    )
```

```python
import functools
import math

import jax
import jax.numpy as jnp
from jax import lax
from jax.experimental import pallas as pl
from jax.experimental.pallas import tpu as pltpu
from jax.sharding import PartitionSpec as P

HEADS = 4
DIM = 128
TOK = 256
LINE = 4
RING = 8
BEHIND = 7
BAND = 12
OWN = 8
PART = 64
MASKED = -1e30
F32 = jnp.float32
BF16 = jnp.bfloat16
VMEM = pl.BlockSpec(memory_space=pltpu.VMEM)
SMEM = pl.BlockSpec(memory_space=pltpu.SMEM)
AXES = ("seq", "dp")


def routes(seq, dp):
    rings = seq // RING
    last, before_last = [], []
    for ring in range(rings):
        for y in range(RING):
            for part in range(dp):
                me = (ring * RING + y) * dp + part
                ahead = ring + (y >= LINE)
                if ahead < rings:
                    last.append((me, (ahead * RING + RING - 1 - y) * dp + part))
                if ring + 1 < rings:
                    before_last.append((me, me + RING * dp))
    return last, before_last


def reverse(route):
    return [(b, a) for a, b in route]


def head_columns(flip, place):
    head = jnp.where(flip == 1, HEADS - 1 - place, place)
    return pl.ds(pl.multiple_of(head * DIM, DIM), DIM)


def pack_kernel(flip_ref, a_ref, b_ref, c_ref, d_ref, keys_ref, queries_ref):
    for place in range(HEADS):
        columns = head_columns(flip_ref[0], place)
        keys_ref[place, 0] = a_ref[:, columns]
        keys_ref[place, 1] = b_ref[:, columns]
        queries_ref[place, 0] = c_ref[:, columns]
        queries_ref[place, 1] = d_ref[:, columns]


def pack(flip, *states):
    return pl.pallas_call(
        pack_kernel,
        out_shape=[jax.ShapeDtypeStruct((HEADS, 2, TOK, DIM), BF16)] * 2,
        in_specs=[SMEM] + [VMEM] * 4,
        out_specs=[VMEM] * 2,
        cost_estimate=pl.CostEstimate(flops=0, bytes_accessed=2**21, transcendentals=0),
    )(flip, *states)


def starts_kernel(range_ref, seg_ref, start_ref, low_ref):
    first_block = range_ref[0] * LINE

    def ids(block):
        return seg_ref[0:1, pl.ds(pl.multiple_of(block * TOK, TOK), TOK)]

    own = [ids(first_block + j) for j in range(LINE)]
    ahead = [(first_block - b, ids(jnp.maximum(first_block - b, 0))) for b in range(1, BEHIND + 1)]
    counts = []
    for j in range(LINE):
        first = own[j][:, :1]
        same = jnp.zeros((1, TOK), jnp.int32)
        for i in range(j):
            same += (own[i] == first).astype(jnp.int32)
        for block, row in ahead[: BEHIND - j]:
            same += ((row == first) & (block >= 0)).astype(jnp.int32)
        counts.append(same)
    count = jnp.sum(jnp.concatenate(counts, axis=0), axis=1, keepdims=True)
    seg = jnp.concatenate(own, axis=0)
    column = lax.broadcasted_iota(jnp.int32, (LINE, TOK), 1)
    begin = jnp.where(seg != pltpu.roll(seg, 1, 1), column, 0)
    begin = jnp.where(column == 0, 0, begin)
    step = 1
    while step < TOK:
        begin = jnp.maximum(begin, jnp.where(column >= step, pltpu.roll(begin, step, 1), 0))
        step *= 2
    block_at = (OWN + lax.broadcasted_iota(jnp.int32, (LINE, TOK), 0)) * TOK
    start = block_at + jnp.where(begin > 0, begin, -count)
    start_ref[...] = start
    for j in range(LINE):
        low_ref[j] = jnp.min(start[j : j + 1, :])


def starts(range_index, seg):
    return pl.pallas_call(
        starts_kernel,
        out_shape=[jax.ShapeDtypeStruct((LINE, TOK), jnp.int32), jax.ShapeDtypeStruct((LINE,), jnp.int32)],
        in_specs=[SMEM, VMEM],
        out_specs=[VMEM, SMEM],
        cost_estimate=pl.CostEstimate(flops=0, bytes_accessed=2**20, transcendentals=0),
    )(range_index, seg)


def unpack_kernel(flip_ref, dq_ref, dk_ref, query_ref, key_ref):
    for place in range(HEADS):
        columns = head_columns(flip_ref[0], place)
        query_ref[:, columns] = dq_ref[place].astype(F32)
        key_ref[:, columns] = dk_ref[place].astype(F32)


def unpack(flip, dq, dk):
    return pl.pallas_call(
        unpack_kernel,
        out_shape=[jax.ShapeDtypeStruct((TOK, HEADS * DIM), F32)] * 2,
        in_specs=[SMEM, VMEM, VMEM],
        out_specs=[VMEM] * 2,
        cost_estimate=pl.CostEstimate(flops=0, bytes_accessed=12 * TOK * 512, transcendentals=0),
    )(flip, dq, dk)


def layout_kernel(own_ref, last_ref, before_ref, kt, ks):
    def load(block, teacher, student):
        here = pl.ds(block * TOK, TOK)
        kt[here, :] = teacher
        ks[here, :] = student

    load(0, jnp.zeros((TOK, DIM), BF16), jnp.zeros((TOK, DIM), BF16))
    for i in range(LINE - 1):
        load(1 + i, before_ref[i, 0], before_ref[i, 1])
    for i in range(LINE):
        load(LINE + i, last_ref[i, 0], last_ref[i, 1])
        load(OWN + i, own_ref[i, 0], own_ref[i, 1])


def layout(own, last, before):
    return pl.pallas_call(
        layout_kernel,
        out_shape=[
            jax.ShapeDtypeStruct((BAND * TOK, DIM), BF16),
            jax.ShapeDtypeStruct((BAND * TOK, DIM), BF16),
        ],
        in_specs=[VMEM] * 3,
        out_specs=[VMEM] * 2,
        compiler_params=pltpu.CompilerParams(vmem_limit_bytes=6 * 1024 * 1024),
        cost_estimate=pl.CostEstimate(flops=10**10, bytes_accessed=16 * 2**20, transcendentals=0),
    )(own, last, before)


def main_kernel(
    head_ref, low_ref, weight_ref, start_ref, query_ref, kt, ks,
    dq_ref, dk_own_ref, dk_last_ref, dk_before_ref,
    ks_turned, dk, et, es, grad, top_t, top_s, sum_t, sum_s, factor_t, factor_s,
):
    weight = weight_ref[head_ref[0]]
    scale = 1.0 / math.sqrt(DIM)
    pace = scale * math.log2(math.e)
    lowest = low_ref[0] // TOK

    def rows(block):
        return pl.ds(block * TOK, TOK)

    dk[...] = jnp.zeros((BAND * TOK, DIM), F32)
    for block in range(BAND):
        @pl.when(block >= lowest - 1)
        def _():
            ks_turned[:, rows(block)] = ks[rows(block), :].T

    def work(j, blocks):
        base = pl.multiple_of((OWN + j + 1 - blocks) * TOK, TOK)
        q_t, q_s = query_ref[j, 0], query_ref[j, 1]
        sides = (
            (kt, q_t.T, et, top_t, sum_t, factor_t),
            (ks, q_s.T, es, top_s, sum_s, factor_s),
        )
        start = start_ref[pl.ds(j, 1), :] - base
        key_row = lax.broadcasted_iota(jnp.int32, (PART, TOK), 0)
        query_column = lax.broadcasted_iota(jnp.int32, (PART, TOK), 1)
        parts = [(i, c) for i in range(blocks) for c in range(TOK // PART)]
        held = pl.ds(0, len(parts))

        span = pl.ds(base, blocks * TOK)

        scores = [jnp.dot(k[span, :], q, preferred_element_type=F32) for k, q, *_ in sides]
        for i in range(blocks):
            for c in range(TOK // PART):
                here, at = pl.ds(c * PART, PART), i * (TOK // PART) + c
                visible = key_row >= start - (i * TOK + c * PART)
                if i == blocks - 1:
                    visible = visible & (key_row <= query_column - c * PART)
                for s, (_, _, e, top, total, _) in zip(scores, sides):
                    x = jnp.where(visible, s[at * PART : (at + 1) * PART], MASKED)
                    h = jnp.max(x, axis=0, keepdims=True)
                    x = jnp.exp2((x - h) * pace)
                    e[i, here, :] = x
                    top[pl.ds(at, 1), :] = h
                    total[pl.ds(at, 1), :] = jnp.sum(x, axis=0, keepdims=True)
        for _, _, _, top, total, factor in sides:
            tops = top[held, :]
            f = jnp.exp2((tops - jnp.max(tops, axis=0, keepdims=True)) * pace)
            factor[held, :] = f * (weight / jnp.sum(total[held, :] * f, axis=0, keepdims=True))
        for i in range(blocks):
            for c in range(TOK // PART):
                here, at = pl.ds(c * PART, PART), pl.ds(i * (TOK // PART) + c, 1)
                g = es[i, here, :] * factor_s[at, :] - et[i, here, :] * factor_t[at, :]
                grad[pl.ds(i * TOK + c * PART, PART), :] = g.astype(BF16)
        grads = grad[: blocks * TOK, :]
        dk[span, :] += jnp.dot(grads, q_s, preferred_element_type=F32)
        dq = jnp.dot(ks_turned[:, span], grads, preferred_element_type=F32)
        dq_ref[j] = (dq * scale).T.astype(BF16)

    def query_block(j, _):
        pairs = (OWN + j + 2 - low_ref[j] // TOK) // 2
        for p in range(1, LINE + 1):
            @pl.when(pairs == p)
            def _():
                work(j, 2 * p)

        return 0

    lax.fori_loop(0, LINE, query_block, 0)

    for i in range(LINE):
        dk_own_ref[i] = dk[rows(OWN + i), :] * scale
        dk_last_ref[i] = (dk[rows(LINE + i), :] * scale).astype(BF16)
    for i in range(LINE - 1):
        dk_before_ref[i] = (dk[rows(1 + i), :] * scale).astype(BF16)


def attend(head, low, weight, start, queries, *keys):
    return pl.pallas_call(
        main_kernel,
        out_shape=[
            jax.ShapeDtypeStruct((LINE, TOK, DIM), BF16),
            jax.ShapeDtypeStruct((LINE, TOK, DIM), F32),
            jax.ShapeDtypeStruct((LINE, TOK, DIM), BF16),
            jax.ShapeDtypeStruct((LINE - 1, TOK, DIM), BF16),
        ],
        in_specs=[SMEM] * 3 + [VMEM] * 4,
        out_specs=[VMEM] * 4,
        scratch_shapes=[
            pltpu.VMEM((DIM, BAND * TOK), BF16),
            pltpu.VMEM((BAND * TOK, DIM), F32),
            pltpu.VMEM((OWN, TOK, TOK), F32),
            pltpu.VMEM((OWN, TOK, TOK), F32),
            pltpu.VMEM((OWN * TOK, TOK), BF16),
        ]
        + [pltpu.VMEM((OWN * TOK // PART, TOK), F32)] * 6,
        compiler_params=pltpu.CompilerParams(vmem_limit_bytes=20 * 1024 * 1024),
        cost_estimate=pl.CostEstimate(flops=10**9, bytes_accessed=6 * 2**20, transcendentals=4 * 10**6),
    )(head, low, weight, start, queries, *keys)


def per_device(seq, dp, teacher_query, teacher_key, student_query, student_key, segment_ids, head_weight):
    to_next, to_second = routes(seq, dp)
    lines = [list(range(i, i + LINE)) for i in range(0, seq, LINE)]
    seq_index = lax.axis_index("seq")
    range_index = seq_index // LINE
    flip = lax.rem(range_index, 2)
    place = lax.rem(seq_index, LINE)
    head = jnp.where(flip == 1, HEADS - 1 - place, place)

    def move(x, route):
        return lax.ppermute(x, AXES, route)

    def exchange(x):
        return lax.all_to_all(x, "seq", 0, 0, axis_index_groups=lines)

    flip, range_index, head = flip.reshape(1), range_index.reshape(1), head.reshape(1)
    keys, queries = pack(flip, teacher_key[0], student_key[0], teacher_query[0], student_query[0])
    own = exchange(keys)
    last = move(own, to_next)
    before = move(own[1:], to_second)
    start, low = starts(range_index, segment_ids)
    queries = exchange(queries)
    dq, dk_own, dk_last, dk_before = attend(head, low, head_weight, start, queries, *layout(own, last, before))

    back_last = move(dk_last, reverse(to_next)).astype(F32)
    back_before = move(dk_before, reverse(to_second)).astype(F32)
    dq_home = exchange(dq)
    total = dk_own + back_last + jnp.pad(back_before, ((1, 0), (0, 0), (0, 0)))
    query_grad, key_grad = unpack(flip, dq_home, exchange(total.astype(BF16)))
    return query_grad[None], key_grad[None]


def solution(mesh):
    seq, dp = mesh.shape["seq"], mesh.shape["dp"]
    spec = P("dp", "seq", None)
    return jax.shard_map(
        functools.partial(per_device, seq, dp),
        mesh=mesh,
        in_specs=(spec, spec, spec, spec, P("dp", None), P()),
        out_specs=(spec, spec),
        check_vma=False,
    )
```

```python
import functools
import math

import jax
import jax.numpy as jnp
from jax import lax
from jax.experimental import pallas as pl
from jax.experimental.pallas import tpu as pltpu
from jax.sharding import PartitionSpec as P

HEADS = 4
DIM = 128
TOK = 256
LINE = 4
RING = 8
BEHIND = 7
BAND = 12
OWN = 8
PART = 64
MASKED = -1e30
F32 = jnp.float32
BF16 = jnp.bfloat16
VMEM = pl.BlockSpec(memory_space=pltpu.VMEM)
SMEM = pl.BlockSpec(memory_space=pltpu.SMEM)
AXES = ("seq", "dp")


def routes(seq, dp):
    rings = seq // RING
    last, before_last = [], []
    for ring in range(rings):
        for y in range(RING):
            for part in range(dp):
                me = (ring * RING + y) * dp + part
                ahead = ring + (y >= LINE)
                if ahead < rings:
                    last.append((me, (ahead * RING + RING - 1 - y) * dp + part))
                if ring + 1 < rings:
                    before_last.append((me, me + RING * dp))
    return last, before_last


def reverse(route):
    return [(b, a) for a, b in route]


def head_columns(flip, place):
    head = jnp.where(flip == 1, HEADS - 1 - place, place)
    return pl.ds(pl.multiple_of(head * DIM, DIM), DIM)


def pack_kernel(flip_ref, a_ref, b_ref, c_ref, d_ref, keys_ref, queries_ref):
    for place in range(HEADS):
        columns = head_columns(flip_ref[0], place)
        keys_ref[place, 0] = a_ref[:, columns]
        keys_ref[place, 1] = b_ref[:, columns]
        queries_ref[place, 0] = c_ref[:, columns]
        queries_ref[place, 1] = d_ref[:, columns]


def pack(flip, *states):
    return pl.pallas_call(
        pack_kernel,
        out_shape=[jax.ShapeDtypeStruct((HEADS, 2, TOK, DIM), BF16)] * 2,
        in_specs=[SMEM] + [VMEM] * 4,
        out_specs=[VMEM] * 2,
        cost_estimate=pl.CostEstimate(flops=0, bytes_accessed=2**21, transcendentals=0),
    )(flip, *states)


def starts_kernel(range_ref, seg_ref, start_ref, low_ref):
    first_block = range_ref[0] * LINE

    def ids(block):
        return seg_ref[0:1, pl.ds(pl.multiple_of(block * TOK, TOK), TOK)]

    own = [ids(first_block + j) for j in range(LINE)]
    ahead = [(first_block - b, ids(jnp.maximum(first_block - b, 0))) for b in range(1, BEHIND + 1)]
    counts = []
    for j in range(LINE):
        first = own[j][:, :1]
        same = jnp.zeros((1, TOK), jnp.int32)
        for i in range(j):
            same += (own[i] == first).astype(jnp.int32)
        for block, row in ahead[: BEHIND - j]:
            same += ((row == first) & (block >= 0)).astype(jnp.int32)
        counts.append(same)
    count = jnp.sum(jnp.concatenate(counts, axis=0), axis=1, keepdims=True)
    seg = jnp.concatenate(own, axis=0)
    column = lax.broadcasted_iota(jnp.int32, (LINE, TOK), 1)
    begin = jnp.where(seg != pltpu.roll(seg, 1, 1), column, 0)
    begin = jnp.where(column == 0, 0, begin)
    step = 1
    while step < TOK:
        begin = jnp.maximum(begin, jnp.where(column >= step, pltpu.roll(begin, step, 1), 0))
        step *= 2
    block_at = (OWN + lax.broadcasted_iota(jnp.int32, (LINE, TOK), 0)) * TOK
    start = block_at + jnp.where(begin > 0, begin, -count)
    start_ref[...] = start
    for j in range(LINE):
        low_ref[j] = jnp.min(start[j : j + 1, :])


def starts(range_index, seg):
    return pl.pallas_call(
        starts_kernel,
        out_shape=[jax.ShapeDtypeStruct((LINE, TOK), jnp.int32), jax.ShapeDtypeStruct((LINE,), jnp.int32)],
        in_specs=[SMEM, VMEM],
        out_specs=[VMEM, SMEM],
        cost_estimate=pl.CostEstimate(flops=0, bytes_accessed=2**20, transcendentals=0),
    )(range_index, seg)


def unpack_kernel(flip_ref, grads_ref, query_ref, key_ref):
    for place in range(HEADS):
        columns = head_columns(flip_ref[0], place)
        query_ref[:, columns] = grads_ref[place, 0].astype(F32)
        key_ref[:, columns] = grads_ref[place, 1].astype(F32)


def unpack(flip, grads):
    return pl.pallas_call(
        unpack_kernel,
        out_shape=[jax.ShapeDtypeStruct((TOK, HEADS * DIM), F32)] * 2,
        in_specs=[SMEM, VMEM],
        out_specs=[VMEM] * 2,
        cost_estimate=pl.CostEstimate(flops=0, bytes_accessed=12 * TOK * 512, transcendentals=0),
    )(flip, grads)


def layout_kernel(own_ref, last_ref, before_ref, kt, ks):
    def load(block, teacher, student):
        here = pl.ds(block * TOK, TOK)
        kt[here, :] = teacher
        ks[here, :] = student

    load(0, jnp.zeros((TOK, DIM), BF16), jnp.zeros((TOK, DIM), BF16))
    for i in range(LINE - 1):
        load(1 + i, before_ref[i, 0], before_ref[i, 1])
    for i in range(LINE):
        load(LINE + i, last_ref[i, 0], last_ref[i, 1])
        load(OWN + i, own_ref[i, 0], own_ref[i, 1])


def layout(own, last, before):
    return pl.pallas_call(
        layout_kernel,
        out_shape=[
            jax.ShapeDtypeStruct((BAND * TOK, DIM), BF16),
            jax.ShapeDtypeStruct((BAND * TOK, DIM), BF16),
        ],
        in_specs=[VMEM] * 3,
        out_specs=[VMEM] * 2,
        compiler_params=pltpu.CompilerParams(vmem_limit_bytes=6 * 1024 * 1024),
        cost_estimate=pl.CostEstimate(flops=10**10, bytes_accessed=16 * 2**20, transcendentals=0),
    )(own, last, before)


def main_kernel(
    head_ref, low_ref, weight_ref, start_ref, query_ref, kt, ks,
    dq_ref, dk_own_ref, dk_last_ref, dk_before_ref,
    ks_turned, dk, et, es, grad, top_t, top_s, sum_t, sum_s, factor_t, factor_s,
):
    weight = weight_ref[head_ref[0]]
    scale = 1.0 / math.sqrt(DIM)
    pace = scale * math.log2(math.e)
    lowest = low_ref[0] // TOK

    def rows(block):
        return pl.ds(block * TOK, TOK)

    dk[...] = jnp.zeros((BAND * TOK, DIM), F32)
    for block in range(BAND):
        @pl.when(block >= lowest - 1)
        def _():
            ks_turned[:, rows(block)] = ks[rows(block), :].T

    def work(j, blocks):
        base = pl.multiple_of((OWN + j + 1 - blocks) * TOK, TOK)
        q_t, q_s = query_ref[j, 0], query_ref[j, 1]
        sides = (
            (kt, q_t.T, et, top_t, sum_t, factor_t),
            (ks, q_s.T, es, top_s, sum_s, factor_s),
        )
        start = start_ref[pl.ds(j, 1), :] - base
        key_row = lax.broadcasted_iota(jnp.int32, (PART, TOK), 0)
        query_column = lax.broadcasted_iota(jnp.int32, (PART, TOK), 1)
        parts = [(i, c) for i in range(blocks) for c in range(TOK // PART)]
        held = pl.ds(0, len(parts))

        span = pl.ds(base, blocks * TOK)

        scores = [jnp.dot(k[span, :], q, preferred_element_type=F32) for k, q, *_ in sides]
        for i in range(blocks):
            for c in range(TOK // PART):
                here, at = pl.ds(c * PART, PART), i * (TOK // PART) + c
                visible = key_row >= start - (i * TOK + c * PART)
                if i == blocks - 1:
                    visible = visible & (key_row <= query_column - c * PART)
                for s, (_, _, e, top, total, _) in zip(scores, sides):
                    x = jnp.where(visible, s[at * PART : (at + 1) * PART], MASKED)
                    h = jnp.max(x, axis=0, keepdims=True)
                    x = jnp.exp2((x - h) * pace)
                    e[i, here, :] = x
                    top[pl.ds(at, 1), :] = h
                    total[pl.ds(at, 1), :] = jnp.sum(x, axis=0, keepdims=True)
        for _, _, _, top, total, factor in sides:
            tops = top[held, :]
            f = jnp.exp2((tops - jnp.max(tops, axis=0, keepdims=True)) * pace)
            factor[held, :] = f * (weight / jnp.sum(total[held, :] * f, axis=0, keepdims=True))
        for i in range(blocks):
            for c in range(TOK // PART):
                here, at = pl.ds(c * PART, PART), pl.ds(i * (TOK // PART) + c, 1)
                g = es[i, here, :] * factor_s[at, :] - et[i, here, :] * factor_t[at, :]
                grad[pl.ds(i * TOK + c * PART, PART), :] = g.astype(BF16)
        grads = grad[: blocks * TOK, :]
        dk[span, :] += jnp.dot(grads, q_s, preferred_element_type=F32)
        dq = jnp.dot(ks_turned[:, span], grads, preferred_element_type=F32)
        dq_ref[j] = (dq * scale).T.astype(BF16)

    def query_block(j, _):
        pairs = (OWN + j + 2 - low_ref[j] // TOK) // 2
        for p in range(1, LINE + 1):
            @pl.when(pairs == p)
            def _():
                work(j, 2 * p)

        return 0

    lax.fori_loop(0, LINE, query_block, 0)

    for i in range(LINE):
        dk_own_ref[i] = dk[rows(OWN + i), :] * scale
        dk_last_ref[i] = (dk[rows(LINE + i), :] * scale).astype(BF16)
    for i in range(LINE - 1):
        dk_before_ref[i] = (dk[rows(1 + i), :] * scale).astype(BF16)


def attend(head, low, weight, start, queries, *keys):
    return pl.pallas_call(
        main_kernel,
        out_shape=[
            jax.ShapeDtypeStruct((LINE, TOK, DIM), BF16),
            jax.ShapeDtypeStruct((LINE, TOK, DIM), F32),
            jax.ShapeDtypeStruct((LINE, TOK, DIM), BF16),
            jax.ShapeDtypeStruct((LINE - 1, TOK, DIM), BF16),
        ],
        in_specs=[SMEM] * 3 + [VMEM] * 4,
        out_specs=[VMEM] * 4,
        scratch_shapes=[
            pltpu.VMEM((DIM, BAND * TOK), BF16),
            pltpu.VMEM((BAND * TOK, DIM), F32),
            pltpu.VMEM((OWN, TOK, TOK), F32),
            pltpu.VMEM((OWN, TOK, TOK), F32),
            pltpu.VMEM((OWN * TOK, TOK), BF16),
        ]
        + [pltpu.VMEM((OWN * TOK // PART, TOK), F32)] * 6,
        compiler_params=pltpu.CompilerParams(vmem_limit_bytes=20 * 1024 * 1024),
        cost_estimate=pl.CostEstimate(flops=10**9, bytes_accessed=6 * 2**20, transcendentals=4 * 10**6),
    )(head, low, weight, start, queries, *keys)


def per_device(seq, dp, teacher_query, teacher_key, student_query, student_key, segment_ids, head_weight):
    to_next, to_second = routes(seq, dp)
    lines = [list(range(i, i + LINE)) for i in range(0, seq, LINE)]
    seq_index = lax.axis_index("seq")
    range_index = seq_index // LINE
    flip = lax.rem(range_index, 2)
    place = lax.rem(seq_index, LINE)
    head = jnp.where(flip == 1, HEADS - 1 - place, place)

    def move(x, route):
        return lax.ppermute(x, AXES, route)

    def exchange(x):
        return lax.all_to_all(x, "seq", 0, 0, axis_index_groups=lines)

    flip, range_index, head = flip.reshape(1), range_index.reshape(1), head.reshape(1)
    keys, queries = pack(flip, teacher_key[0], student_key[0], teacher_query[0], student_query[0])
    own = exchange(keys)
    last = move(own, to_next)
    before = move(own[1:], to_second)
    start, low = starts(range_index, segment_ids)
    queries = exchange(queries)
    dq, dk_own, dk_last, dk_before = attend(head, low, head_weight, start, queries, *layout(own, last, before))

    back_last = move(dk_last, reverse(to_next)).astype(F32)
    back_before = move(dk_before, reverse(to_second)).astype(F32)
    total = dk_own + back_last + jnp.pad(back_before, ((1, 0), (0, 0), (0, 0)))
    query_grad, key_grad = unpack(flip, exchange(jnp.stack([dq, total.astype(BF16)], axis=1)))
    return query_grad[None], key_grad[None]


def solution(mesh):
    seq, dp = mesh.shape["seq"], mesh.shape["dp"]
    spec = P("dp", "seq", None)
    return jax.shard_map(
        functools.partial(per_device, seq, dp),
        mesh=mesh,
        in_specs=(spec, spec, spec, spec, P("dp", None), P()),
        out_specs=(spec, spec),
        check_vma=False,
    )
```
